256 devices in a mesh: dp: 32 (over z, y), tensor: 8 (over x, core).
Axes of the slice: x: 4, y: 4, z: 8, core: 2. Of those that a mesh axis runs over, the one named last changes fastest.
Arguments:
- queries: bfloat16 [512, 64, 4096], P('dp', 'tensor'), may hold values from -130 to 130
- enc_hidden: bfloat16 [128, 128, 8192], P('dp'), may hold values from -400 to 400
- enc_gain: bfloat16 [8192], replicated, may hold values from 0.099609375 to 1.8984375
- kv_weight: bfloat16 [8192, 2, 4096], P('dp', None, 'tensor'), may hold values from -0.0625 to 0.0625
- neighbour_pages: int32 [512, 2], P('dp'), may hold values from 0 to 127, as said below
- reader_counts: int32 [32, 128], P('dp'), may hold values 0 or 1
- neighbour_tokens: int32 [128, 128], P('dp'), may hold values from 0 to 31999, as said below
Outputs:
- context: bfloat16 [512, 64, 4096], P('dp', 'tensor')
- kept_pages: bfloat16 [128, 128, 2, 4096], P('dp', None, None, 'tensor')
The draws below stay inside these ranges and needn't reach their ends.
Inputs may be any that keep to these rules, and one draw needn't show every extreme that they name: `neighbour_pages`: entry (c, n) names slot page % 4 of owner page // 4, an index along dp. The groups of one dp index name pages of exactly 17 distinct owners and never two different pages of one owner; neighbour 1 of such a group c equals neighbour 0 of the same index's group c + 1, and the two neighbours of a group differ. `neighbour_tokens`: 0 marks padding: the zeros of a page are exactly its positions from its length on, a length of 64 to 128.
All inputs are finite; a program needn't handle non-finite values. No bound on the sum of `reader_counts` on one device may be relied on, other than what follows from the above.
Results may differ from the reference program's by a relative error of at most 0.0075.
Values may be sent and summed in bfloat16 or wider, within the bound.
A program may use at most 128 MiB of HBM per device.

```python
import jax
import jax.numpy as jnp
from jax import lax

D = 8192
HEAD = 128
HEADS = 32
HD = 4096
GROUP = 64
NB_TOK = 128
NBRS = 2
GROUPS_DEV = 16
PAGES_DEV = 4
READERS = 32
GROUPS = 512
PAGES = 128


def shuffled(seed_key):
    return jax.random.permutation(seed_key, READERS)


def draw_queries(key, part):
    key = jax.random.fold_in(key, 11)
    return jnp.clip(jax.random.normal(key, (GROUPS, GROUP, HD), jnp.float32), -6.0, 6.0).astype(jnp.bfloat16)


def draw_enc_hidden(key, part):
    key = jax.random.fold_in(key, 12)
    value_key, row_key, column_key = jax.random.split(key, 3)
    row_scale = jnp.exp(jax.random.uniform(row_key, (PAGES, NB_TOK, 1), jnp.float32, 0.0, 2.3))
    column_scale = jnp.exp(jax.random.uniform(column_key, (1, 1, D), jnp.float32, 0.0, 2.3))
    normal_part = jnp.clip(jax.random.normal(value_key, (PAGES, NB_TOK, D), jnp.float32), -4.0, 4.0)
    return (normal_part * row_scale * column_scale).astype(jnp.bfloat16)


def draw_neighbour_pages(key, part):
    key = jax.random.fold_in(key, 13)
    perm_key, slot_key = jax.random.split(key)
    orders = jax.vmap(shuffled)(jax.random.split(perm_key, READERS))
    first_owner = orders[:, :1]
    goal_owner = jnp.zeros((READERS, 1), jnp.int32).at[0, 0].set(READERS - 1)
    orders = (orders - first_owner + goal_owner) % READERS
    slot_table = jax.random.randint(slot_key, (READERS, READERS), 0, PAGES_DEV)
    slot_table = slot_table.at[0, 0].set(PAGES_DEV - 1).at[1, 0].set(0)
    spread = min(READERS, GROUPS_DEV + 1)
    group_index = jnp.arange(GROUPS_DEV, dtype=jnp.int32)
    uniques = jnp.stack([group_index % spread, (group_index + 1) % spread], axis=1)
    owner_ids = jnp.take(orders, uniques, axis=1)
    slot_ids = jnp.take(slot_table, uniques, axis=1)
    return (owner_ids * PAGES_DEV + slot_ids).reshape(GROUPS, NBRS).astype(jnp.int32)


def draw_neighbour_tokens(key, part):
    key = jax.random.fold_in(key, 14)
    id_key, length_key = jax.random.split(key)
    token_ids = jax.random.randint(id_key, (PAGES, NB_TOK), 1, 32000)
    lengths = jax.random.randint(length_key, (PAGES, 1), GROUP, NB_TOK + 1)
    lengths = lengths.at[0, 0].set(GROUP)
    position = lax.broadcasted_iota(jnp.int32, (PAGES, NB_TOK), 1)
    token_ids = jnp.where(position < lengths, token_ids, 0)
    return token_ids.at[0, 0].set(31999).astype(jnp.int32)


def touch_ends(values, key, least, largest):
    longest = values.shape.index(max(values.shape))
    spots = []
    for shift in (0, 1):
        where = [jax.random.randint(jax.random.fold_in(key, axis), (), 0, length) for axis, length in enumerate(values.shape)]
        where[longest] = (where[longest] + shift) % values.shape[longest]
        spots.append(tuple(where))
    return values.at[spots[0]].set(least).at[spots[1]].set(largest)


def steps_of(own_key, dims, cuts, least, top_value):
    loudness = 1.0
    for axis_at, shards_of in cuts:
        steps = jax.random.uniform(jax.random.fold_in(jax.random.fold_in(own_key, 6), axis_at), (shards_of,), jnp.float32, least / len(cuts), top_value / len(cuts))
        loudness = loudness * jnp.repeat(jnp.exp(steps), dims[axis_at] // shards_of).reshape((-1,) + (1,) * (len(dims) - 1 - axis_at))
    return loudness


def scatter_about(key, extent, scale, reach, cuts=(), kind=jnp.bfloat16):
    drawn = jax.random.normal(key, extent, jnp.float32) * scale
    if len(cuts) > 0:
        drawn = steps_of(key, extent, cuts, -0.22, 0.18) * drawn
    return jnp.clip(drawn, min=-reach, max=reach).astype(kind)


def setup_inputs(seed: int = 0) -> dict:
    key_list = jax.random.split(jax.random.key(seed), 8)
    queries = draw_queries(jax.random.fold_in(key_list[7], 71), 0)
    enc_hidden = draw_enc_hidden(jax.random.fold_in(key_list[7], 71), 0)
    enc_gain = jnp.clip(1.0 + 0.18 * jax.random.normal(key_list[2], (D,), jnp.float32), 0.099609375, 1.8984375).astype(jnp.bfloat16)
    kv_weight = scatter_about(key_list[3], (D, 2, HD), D ** -0.5, 0.0625, ((0, 32), (2, 8)))
    neighbour_pages = draw_neighbour_pages(jax.random.fold_in(key_list[7], 71), 0)
    reader_counts = touch_ends((jax.random.randint(key_list[5], (READERS, PAGES), 0, 16) < 1).astype(jnp.int32), jax.random.fold_in(key_list[5], 1), 0, 1)
    neighbour_tokens = draw_neighbour_tokens(jax.random.fold_in(key_list[7], 71), 0)
    return {"queries": queries, "enc_hidden": enc_hidden, "enc_gain": enc_gain, "kv_weight": kv_weight, "neighbour_pages": neighbour_pages, "reader_counts": reader_counts, "neighbour_tokens": neighbour_tokens}


epsilon = 1e-05
masked_score = -1e+30

def reference(queries, enc_hidden, enc_gain, kv_weight, neighbour_pages, reader_counts, neighbour_tokens):
    hidden = enc_hidden.astype(jnp.float32)
    inverse = lax.rsqrt(lax.optimization_barrier(jnp.mean(hidden * hidden, axis=-1, keepdims=True)) + epsilon)
    normed = (hidden * inverse * enc_gain.astype(jnp.float32)).astype(jnp.bfloat16)
    flat_rows = normed.reshape(PAGES * NB_TOK, D)
    projected = jnp.dot(flat_rows, kv_weight.reshape(D, 2 * HD), preferred_element_type=jnp.float32)
    pages = projected.astype(jnp.bfloat16).reshape(PAGES, NB_TOK, 2, HD)
    totals = lax.optimization_barrier(jnp.sum(reader_counts, axis=0))
    kept_pages = jnp.where((totals > 0)[:, None, None, None], pages, jnp.zeros_like(pages))

    def one_group(operands):
        group_queries, page_pair = operands
        stacked = pages[page_pair].reshape(NBRS * NB_TOK, 2, HEADS, HEAD)
        token_ids = neighbour_tokens[page_pair].reshape(NBRS * NB_TOK)
        query_rows = group_queries.reshape(GROUP, HEADS, HEAD).astype(jnp.float32)
        key_rows = stacked[:, 0].astype(jnp.float32)
        value_rows = stacked[:, 1].astype(jnp.float32)
        scores = jnp.einsum('ihe,jhe->hij', query_rows, key_rows) * HEAD ** (-0.5)
        scores = jnp.where((token_ids != 0)[None, None, :], scores, masked_score)
        row_max = lax.optimization_barrier(jnp.max(scores, axis=-1, keepdims=True))
        weights = jnp.exp(scores - row_max)
        softmax_weights = (weights / lax.optimization_barrier(jnp.sum(weights, axis=-1, keepdims=True))).astype(jnp.bfloat16)
        mixed = jnp.einsum('hij,jhe->ihe', softmax_weights.astype(jnp.float32), value_rows)
        return mixed.astype(jnp.bfloat16).reshape(GROUP, HD)
    context = lax.map(one_group, (queries, neighbour_pages))
    return (context, kept_pages)
```

```python
import functools

import jax
import jax.numpy as jnp
from jax import lax
from jax.experimental import pallas as pl
from jax.experimental.pallas import tpu as pltpu
from jax.sharding import PartitionSpec as P

HEAD = 128
GROUP = 64
NBRS = 2
Z, Y, X, C = 8, 4, 4, 2
T = X * C
MESH = pl.DeviceIdType.MESH

epsilon = 1e-05
masked_score = -1e30


def place():
    dp = lax.axis_index("dp")
    t = lax.axis_index("tensor")
    return dp // Y, dp % Y, t // C, t % C


def remote(src, dst, send, recv, z, y, x, c):
    return pltpu.make_async_remote_copy(
        src_ref=src,
        dst_ref=dst,
        send_sem=send,
        recv_sem=recv,
        device_id=(z * Y + y, x * C + c),
        device_id_type=MESH,
    )


def greet(peers):
    barrier = pltpu.get_barrier_semaphore()
    for z, y, x, c in peers:
        pl.semaphore_signal(barrier, inc=1, device_id=(z * Y + y, x * C + c), device_id_type=MESH)
    pl.semaphore_wait(barrier, len(peers))


def greet_plane(also=()):
    z, y, x, c = place()
    me = y * T + x * C + c
    barrier = pltpu.get_barrier_semaphore()

    @pl.loop(1, Y * T)
    def _(k):
        p = (me + k) % (Y * T)
        pl.semaphore_signal(barrier, inc=1, device_id=(z * Y + p // T, p % T), device_id_type=MESH)

    for pz, py, px, pc in also:
        pl.semaphore_signal(barrier, inc=1, device_id=(pz * Y + py, px * C + pc), device_id_type=MESH)
    pl.semaphore_wait(barrier, Y * T - 1 + len(also))


def hop_counts(n, c):
    far, near = n // 2, n - 1 - n // 2
    return (far, near) if c % 2 == 0 else (near, far)


def gather_kernel(
    w, act, q, meta, wfull, afull, qfull, mfull,
    lsem, wsend, wrecv, asend, arecv, xsend, xrecv, csend, crecv, qsend, qrecv, msend, mrecv, nsend, nrecv,
):
    z, y, x, c = place()
    t = x * C + c
    half = w.shape[0] // 2
    greet_plane([((z + k) % Z, y, x, c) for k in range(1, Z)])
    locals_ = []
    sends = []

    def local(src, dst):
        cp = pltpu.make_async_copy(src, dst, lsem.at[len(locals_)])
        cp.start()
        locals_.append(cp)
        return cp

    def zpeer(d, h):
        return (z + h) % Z if d == 0 else (z + Z - h) % Z

    def xpeer(d, h):
        return (x + h) % X if d == 0 else (x + X - h) % X

    def wcopy(d, h, k):
        src_z = zpeer(1 - d, h - 1)
        rows = pl.ds(k * half, half)
        src = w.at[rows] if h == 1 else wfull.at[src_z, rows]
        return remote(src, wfull.at[src_z, rows], wsend.at[d, h - 1, k], wrecv.at[d, h - 1, k], zpeer(d, 1), y, x, c)

    def ypiece(k):
        return (y + k) % Y

    def xcopy(d, h, k):
        src_x = xpeer(1 - d, h - 1)
        yy = ypiece(k)
        src = act.at[y] if (k == 0 and h == 1) else afull.at[yy, src_x * C + c]
        return remote(src, afull.at[yy, src_x * C + c], xsend.at[d, h - 1, k], xrecv.at[d, h - 1, k], z, y, xpeer(d, 1), c)

    def ccopy(src_x, slot, k):
        yy = ypiece(k)
        src = act.at[y] if (k == 0 and slot == 0) else afull.at[yy, src_x * C + c]
        return remote(src, afull.at[yy, src_x * C + c], csend.at[slot, k], crecv.at[slot, k], z, y, x, 1 - c)

    def go(cp):
        cp.start()
        sends.append(cp)

    for k in range(2):
        for d in range(2):
            go(wcopy(d, 1, k))
    for k in (1, 3, 2):
        dst = (y + k) % Y
        cp = remote(act.at[dst], afull.at[y, t], asend.at[k], arecv.at[k], z, dst, x, c)
        go(cp)
    for d in range(2):
        go(xcopy(d, 1, 0))
    go(ccopy(x, 0, 0))
    local(w, wfull.at[z])
    local(act.at[y], afull.at[y, t])
    local(meta, mfull.at[z * Y + y])
    for k in (1, 3, 2):
        go(remote(meta, mfull.at[z * Y + y], msend.at[k], mrecv.at[k], z, (y + k) % Y, x, c))
    me = y * T + t

    def qcopy(k):
        p = (me + k) % (Y * T)
        py, pt = p // T, p % T
        cols = pl.ds(pl.multiple_of((pt * Y + py) * HEAD, HEAD), HEAD)
        return remote(q.at[:, cols], qfull.at[y, t], qsend.at[k], qrecv.at[k], z, py, pt // C, pt % C)

    @pl.loop(1, Y * T)
    def _(k):
        qcopy(k).start()

    own_cols = pl.ds(pl.multiple_of((t * Y + y) * HEAD, HEAD), HEAD)
    local(q.at[:, own_cols], qfull.at[y, t])

    locals_[1].wait()
    for k in (1, 3, 2):
        remote(act.at[y], afull.at[ypiece(k), t], asend.at[Y - k], arecv.at[Y - k], z, y, x, 1 - c).wait_recv()
        for d in range(2):
            go(xcopy(d, 1, k))
        go(ccopy(x, 0, k))

    locals_[2].wait()
    for k in (1, 3, 2):
        remote(meta, mfull.at[z * Y + (y + k) % Y], msend.at[Y - k], mrecv.at[Y - k], z, y, x, 1 - c).wait_recv()
    for k in range(1, Z):
        mine = mfull.at[pl.ds(z * Y, Y)]
        go(remote(mine, mine, nsend.at[k], nrecv.at[k], (z + k) % Z, y, x, c))

    wevents = [(h, k) for h in range(1, Z // 2 + 1) for k in range(2)]
    xevents = [(h, k) for h in range(1, X // 2 + 1) for k in (0, 1, 3, 2)]
    for i in range(max(len(wevents), len(xevents))):
        if i < len(wevents):
            h, k = wevents[i]
            for d in range(2):
                hops = hop_counts(Z, k)[d]
                if h <= hops:
                    src_z = zpeer(1 - d, h)
                    rows = pl.ds(k * half, half)
                    remote(w.at[rows], wfull.at[src_z, rows], wsend.at[d, h - 1, k], wrecv.at[d, h - 1, k], z, y, x, 1 - c).wait_recv()
                    if h + 1 <= hops:
                        go(wcopy(d, h + 1, k))
        if i < len(xevents):
            h, k = xevents[i]
            for d in range(2):
                hops = hop_counts(X, k)[d]
                if h <= hops:
                    src_x = xpeer(1 - d, h)
                    remote(act.at[y], afull.at[ypiece(k), src_x * C + c], xsend.at[d, h - 1, k], xrecv.at[d, h - 1, k], z, y, x, 1 - c).wait_recv()
                    if h + 1 <= hops:
                        go(xcopy(d, h + 1, k))
                    slot = h if d == 0 else X - h
                    go(ccopy(src_x, slot, k))

    for k in (0, 1, 3, 2):
        for slot in range(X):
            src_x = (x + X - slot) % X
            remote(act.at[y], afull.at[ypiece(k), src_x * C + 1 - c], csend.at[slot, k], crecv.at[slot, k], z, y, x, 1 - c).wait_recv()
    for k in range(1, Z):
        theirs = mfull.at[pl.ds(((z + Z - k) % Z) * Y, Y)]
        remote(theirs, theirs, nsend.at[k], nrecv.at[k], z, y, x, 1 - c).wait_recv()

    @pl.loop(1, Y * T)
    def _(k):
        p = (me + Y * T - k) % (Y * T)
        remote(q.at[:, own_cols], qfull.at[p // T, p % T], qsend.at[k], qrecv.at[k], z, y, x, 1 - c).wait_recv()

    @pl.loop(1, Y * T)
    def _(k):
        qcopy(k).wait_send()

    for cp in sends:
        cp.wait_send()
    for i, cp in enumerate(locals_):
        if i not in (1, 2):
            cp.wait()


def gather(w, act, q, meta):
    rows, cols = w.shape
    dma = pltpu.SemaphoreType.DMA
    return pl.pallas_call(
        gather_kernel,
        out_shape=(
            jax.ShapeDtypeStruct((Z, rows, cols), w.dtype),
            jax.ShapeDtypeStruct((Y, T, act.shape[1], act.shape[2]), act.dtype),
            jax.ShapeDtypeStruct((Y, T, q.shape[0], HEAD), q.dtype),
            jax.ShapeDtypeStruct((Z * Y,) + meta.shape, meta.dtype),
        ),
        in_specs=[pl.BlockSpec(memory_space=pl.ANY)] * 4,
        out_specs=[pl.BlockSpec(memory_space=pl.ANY)] * 4,
        scratch_shapes=[
            dma((4,)),
            dma((2, Z // 2, 2)), dma((2, Z // 2, 2)),
            dma((Y,)), dma((Y,)),
            dma((2, X // 2, Y)), dma((2, X // 2, Y)),
            dma((X, Y)), dma((X, Y)),
            dma((Y * T,)), dma((Y * T,)),
            dma((Y,)), dma((Y,)),
            dma((Z,)), dma((Z,)),
        ],
        compiler_params=pltpu.CompilerParams(has_side_effects=True, collective_id=1),
        name="gather",
    )(w, act, q, meta)


ORDER = ((1, 0), (1, 1), (0, 0), (0, 1), (0, 2), (0, 3), (1, 2), (1, 3))


def exchange_kernel(
    kpart, vpart, kpages, vpages, kkept, vkept, krs, vrs, kown, vown,
    lsem, rsend, rrecv, zsend, zrecv, ksend, krecv,
):
    z, y, x, c = place()
    part, pages, kept = (kpart, vpart), (kpages, vpages), (kkept, vkept)
    rs, own = (krs, vrs), (kown, vown)
    chunk = kpart.shape[0] // Y
    greet([(z, (y + k) % Y, x, c) for k in (1, 2, 3)] + [((z + 1) % Z, y, x, c), ((z + Z - 1) % Z, y, x, c)])
    sends = []

    def go(cp):
        cp.start()
        sends.append(cp)

    def zpeer(d, h):
        return (z + h) % Z if d == 0 else (z + Z - h) % Z

    def cols_of(yy):
        return pl.ds(pl.multiple_of(yy * HEAD, HEAD), HEAD)

    def rows_of(m):
        return pl.ds(m * chunk, chunk)

    own_part = {}
    for s, m in ORDER:
        for k in (2, 1, 3):
            dst = (y + k) % Y
            go(remote(part[s].at[rows_of(m), cols_of(dst)], rs[s].at[k, rows_of(m)], rsend.at[s, k, m], rrecv.at[s, k, m], z, dst, x, c))
        cp = pltpu.make_async_copy(part[s].at[rows_of(m), cols_of(y)], rs[s].at[0, rows_of(m)], lsem.at[0, s, m])
        cp.start()
        own_part[s, m] = cp

    def zcopy(d, h, s, m):
        src_z = zpeer(1 - d, h - 1)
        src = own[s].at[rows_of(m)] if h == 1 else pages[s].at[src_z, rows_of(m)]
        return remote(src, pages[s].at[src_z, rows_of(m)], zsend.at[d, h - 1, s, m], zrecv.at[d, h - 1, s, m], zpeer(d, 1), y, x, c)

    def zwait(d, h, s, m):
        src_z = zpeer(1 - d, h)
        remote(own[s].at[rows_of(m)], pages[s].at[src_z, rows_of(m)], zsend.at[d, h - 1, s, m], zrecv.at[d, h - 1, s, m], z, y, x, 1 - c).wait_recv()

    def pass_on(h, s, m):
        for d in range(2):
            hops = hop_counts(Z, m)[d]
            if h <= hops:
                zwait(d, h, s, m)
                if h + 1 <= hops:
                    go(zcopy(d, h + 1, s, m))

    locals_ = []

    def finish(s, m):
        own_part[s, m].wait()
        for k in (1, 3, 2):
            remote(rs[s].at[0, rows_of(m)], rs[s].at[k, rows_of(m)], rsend.at[s, k, m], rrecv.at[s, k, m], z, y, x, 1 - c).wait_recv()
        total = rs[s][0, rows_of(m)].astype(jnp.float32)
        for k in range(1, Y):
            total += rs[s][k, rows_of(m)].astype(jnp.float32)
        own[s][rows_of(m)] = total.astype(own[s].dtype)
        for d in range(2):
            go(zcopy(d, 1, s, m))
        cp = pltpu.make_async_copy(own[s].at[rows_of(m)], pages[s].at[z, rows_of(m)], lsem.at[1, s, m])
        cp.start()
        locals_.append(cp)

        @pl.when(y != m)
        def _():
            remote(own[s].at[rows_of(m)], kept[s].at[y], ksend.at[s, m], krecv.at[s, y], z, m, x, c).start()

        @pl.when(y == m)
        def _():
            pltpu.make_async_copy(own[s].at[rows_of(m)], kept[s].at[y], lsem.at[2, s, m]).start()

    steps = len(ORDER)
    for i in range(steps + Z // 2):
        if i < steps:
            finish(*ORDER[i])
        for h in range(Z // 2, 0, -1):
            if 0 <= i - h < steps:
                pass_on(h, *ORDER[i - h])

    for s, m in ORDER:
        @pl.when(y != m)
        def _():
            remote(own[s].at[rows_of(m)], kept[s].at[m], ksend.at[s, m], krecv.at[s, m], z, y, x, 1 - c).wait()

        @pl.when(y == m)
        def _():
            pltpu.make_async_copy(own[s].at[rows_of(m)], kept[s].at[y], lsem.at[2, s, m]).wait()

    for cp in sends:
        cp.wait_send()
    for cp in locals_:
        cp.wait()


def exchange(kpart, vpart):
    dma = pltpu.SemaphoreType.DMA
    rows = kpart.shape[0]
    pages = jax.ShapeDtypeStruct((Z, rows, HEAD), jnp.bfloat16)
    kept = jax.ShapeDtypeStruct((Y, rows // Y, HEAD), jnp.bfloat16)
    return pl.pallas_call(
        exchange_kernel,
        out_shape=(pages, pages, kept, kept),
        in_specs=[pl.BlockSpec(memory_space=pl.ANY)] * 2,
        out_specs=[pl.BlockSpec(memory_space=pl.ANY)] * 4,
        scratch_shapes=[
            pltpu.VMEM((Y, rows, HEAD), kpart.dtype),
            pltpu.VMEM((Y, rows, HEAD), vpart.dtype),
            pltpu.VMEM((rows, HEAD), jnp.bfloat16),
            pltpu.VMEM((rows, HEAD), jnp.bfloat16),
            dma((3, 2, Y)),
            dma((2, Y, Y)), dma((2, Y, Y)),
            dma((2, Z // 2, 2, Y)), dma((2, Z // 2, 2, Y)),
            dma((2, Y)), dma((2, Y)),
        ],
        compiler_params=pltpu.CompilerParams(has_side_effects=True, collective_id=2, vmem_limit_bytes=32 * 2**20),
        name="exchange",
    )(kpart, vpart)


def attend_kernel(ids, q, kpages, vpages, tokens, out):
    row = lax.broadcasted_iota(jnp.int32, (2 * GROUP, 1), 0)
    second = (row // 8) % 2 == 1

    @pl.loop(0, q.shape[0])
    def _(r):
        @pl.loop(0, q.shape[2] // 16, unroll=True)
        def _(pair):
            span = pl.ds(pair * 16, 16)
            rows_q = q[r, :, span, :].reshape(2 * GROUP, HEAD)
            scores = []
            values = []
            for n in range(3):
                page = ids[r, pair * 4 + (n if n < 2 else 3)]
                keys = kpages[page]
                values.append(vpages[page])
                s = lax.dot_general(rows_q, keys, (((1,), (1,)), ((), ())), preferred_element_type=jnp.float32)
                s = s * HEAD ** (-0.5)
                ok = tokens[pl.ds(page, 1), :] != 0
                if n == 0:
                    ok = jnp.logical_and(ok, jnp.logical_not(second))
                elif n == 2:
                    ok = jnp.logical_and(ok, second)
                scores.append(jnp.where(ok, s, masked_score))
            s = jnp.concatenate(scores, axis=1)
            top = jnp.max(s, axis=1, keepdims=True)
            e = jnp.exp(s - top)
            total = jnp.sum(e, axis=1, keepdims=True)
            probs = (e / total).astype(jnp.bfloat16)
            mixed = jnp.dot(probs, jnp.concatenate(values, axis=0), preferred_element_type=jnp.float32)
            out[r, :, span, :] = mixed.astype(out.dtype).reshape(T, 16, HEAD)


def attend(ids, q, kpages, vpages, tokens):
    return pl.pallas_call(
        attend_kernel,
        out_shape=jax.ShapeDtypeStruct(q.shape, q.dtype),
        in_specs=[pl.BlockSpec(memory_space=pltpu.SMEM)] + [pl.BlockSpec(memory_space=pltpu.VMEM)] * 4,
        out_specs=pl.BlockSpec(memory_space=pltpu.VMEM),
        compiler_params=pltpu.CompilerParams(vmem_limit_bytes=40 * 2**20),
        name="attend",
    )(ids, q, kpages, vpages, tokens)


def give_back_kernel(ctx, out, lsem, send, recv):
    z, y, x, c = place()
    t = x * C + c
    me = y * T + t
    cols = pl.ds(pl.multiple_of((t * Y + y) * HEAD, HEAD), HEAD)
    greet_plane()

    def copy(k):
        p = (me + k) % (Y * T)
        py, pt = p // T, p % T
        return remote(ctx.at[py, pt], out.at[:, cols], send.at[k], recv.at[k], z, py, pt // C, pt % C)

    @pl.loop(1, Y * T)
    def _(k):
        copy(k).start()

    mine = pltpu.make_async_copy(ctx.at[y, t], out.at[:, cols], lsem.at[0])
    mine.start()

    @pl.loop(1, Y * T)
    def _(k):
        p = (me + Y * T - k) % (Y * T)
        py, pt = p // T, p % T
        theirs = pl.ds(pl.multiple_of((pt * Y + py) * HEAD, HEAD), HEAD)
        remote(ctx.at[y, t], out.at[:, theirs], send.at[k], recv.at[k], z, y, x, 1 - c).wait_recv()

    @pl.loop(1, Y * T)
    def _(k):
        copy(k).wait_send()

    mine.wait()


def give_back(ctx):
    dma = pltpu.SemaphoreType.DMA
    return pl.pallas_call(
        give_back_kernel,
        out_shape=jax.ShapeDtypeStruct((ctx.shape[2], Y * T * HEAD), ctx.dtype),
        in_specs=[pl.BlockSpec(memory_space=pl.ANY)],
        out_specs=pl.BlockSpec(memory_space=pl.ANY),
        scratch_shapes=[dma((1,)), dma((Y * T,)), dma((Y * T,))],
        compiler_params=pltpu.CompilerParams(has_side_effects=True, collective_id=3),
        name="give_back",
    )(ctx)


def shards(
    queries, enc_hidden, enc_gain, kv_weight, neighbour_pages, reader_counts, neighbour_tokens
):
    dp = lax.axis_index("dp")
    z, y = dp // Y, dp % Y
    t = lax.axis_index("tensor")
    pages_here, nb_tokens, features = enc_hidden.shape
    groups_here = queries.shape[0]
    k_rows = kv_weight.shape[0]
    rows_here = pages_here * nb_tokens
    share = rows_here // T

    hidden = enc_hidden.reshape(rows_here, features)
    hidden = lax.dynamic_slice_in_dim(hidden, t * share, share, 0).astype(jnp.float32)
    inverse = lax.rsqrt(jnp.mean(hidden * hidden, axis=-1, keepdims=True) + epsilon)
    normed = (hidden * inverse * enc_gain.astype(jnp.float32)).astype(jnp.bfloat16)
    act = normed.reshape(share, Z, Y, k_rows).transpose(2, 0, 1, 3).reshape(Y, share, Z * k_rows)

    w = kv_weight.reshape(k_rows, -1)

    meta = jnp.zeros((8, nb_tokens), jnp.int32)
    meta = meta.at[0].set(reader_counts[0])
    meta = meta.at[1 : 1 + pages_here].set(neighbour_tokens)
    meta = meta.at[1 + pages_here, : groups_here * NBRS].set(neighbour_pages.reshape(-1))

    wfull, afull, qfull, mfull = gather(w, act, queries.reshape(-1, queries.shape[2]), meta)

    rows_k = afull.reshape(Y * rows_here, Z * k_rows)
    w_k = wfull.reshape(Z * k_rows, 2 * Y * HEAD)
    kpart = jnp.dot(rows_k, w_k[:, : Y * HEAD], preferred_element_type=jnp.float32)
    vpart = jnp.dot(rows_k, w_k[:, Y * HEAD :], preferred_element_type=jnp.float32).astype(jnp.bfloat16)
    kpages, vpages, kkept, vkept = exchange(kpart, vpart)

    tokens = mfull[:, 1 : 1 + pages_here].reshape(-1, nb_tokens)
    ids = lax.dynamic_slice_in_dim(mfull[:, 1 + pages_here, : groups_here * NBRS], z * Y, Y, 0)
    by_page = (Z * Y * pages_here, nb_tokens, HEAD)
    ctx = attend(ids, qfull, kpages.reshape(by_page), vpages.reshape(by_page), tokens)
    context = give_back(ctx).reshape(queries.shape)

    totals = lax.dynamic_slice_in_dim(jnp.sum(mfull[:, 0], axis=0), dp * pages_here, pages_here, 0)
    kept = jnp.stack([kkept, vkept]).reshape(2, Y, pages_here, nb_tokens, HEAD).transpose(2, 3, 0, 1, 4)
    kept = kept.reshape(pages_here, nb_tokens, 2, Y * HEAD)
    kept_pages = jnp.where((totals > 0)[:, None, None, None], kept, jnp.zeros_like(kept))
    return (context, kept_pages)


def solution(mesh):
    placed = (
        P("dp", "tensor", None),
        P("dp", None, None),
        P(),
        P("dp", None, "tensor"),
        P("dp", None),
        P("dp", None),
        P("dp", None),
    )
    return jax.shard_map(
        shards,
        mesh=mesh,
        in_specs=placed,
        out_specs=(P("dp", "tensor", None), P("dp", None, None, "tensor")),
        check_vma=False,
    )
```

```python
import functools

import jax
import jax.numpy as jnp
from jax import lax
from jax.experimental import pallas as pl
from jax.experimental.pallas import tpu as pltpu
from jax.sharding import PartitionSpec as P

HEAD = 128
GROUP = 64
NBRS = 2
Z, Y, X, C = 8, 4, 4, 2
T = X * C
MESH = pl.DeviceIdType.MESH

epsilon = 1e-05
masked_score = -1e30


def place():
    dp = lax.axis_index("dp")
    t = lax.axis_index("tensor")
    return dp // Y, dp % Y, t // C, t % C


def remote(src, dst, send, recv, z, y, x, c):
    return pltpu.make_async_remote_copy(
        src_ref=src,
        dst_ref=dst,
        send_sem=send,
        recv_sem=recv,
        device_id=(z * Y + y, x * C + c),
        device_id_type=MESH,
    )


def greet_plane(also=()):
    z, y, x, c = place()
    me = y * T + x * C + c
    barrier = pltpu.get_barrier_semaphore()

    @pl.loop(1, Y * T)
    def _(k):
        p = (me + k) % (Y * T)
        pl.semaphore_signal(barrier, inc=1, device_id=(z * Y + p // T, p % T), device_id_type=MESH)

    for pz, py, px, pc in also:
        pl.semaphore_signal(barrier, inc=1, device_id=(pz * Y + py, px * C + pc), device_id_type=MESH)
    pl.semaphore_wait(barrier, Y * T - 1 + len(also))


def hop_counts(n, c):
    far, near = n // 2, n - 1 - n // 2
    return (far, near) if c % 2 == 0 else (near, far)


KEYS, VALUES = 0, 1
ORIGINS = (0, 1, 3, 2)
ORDER = [(KEYS, j) for j in range(X)] + [(VALUES, j) for j in range(X)]
AHEAD = 2


def layer_kernel(
    enc, gain, w, q, meta, out, kkept, vkept, mout,
    staged, act, afull, wk, wv, ksum, vsum, vmine, krs, vrs, kown, vown, kpages, vpages,
    qfull, probs, ctx, mfull, ids,
    lsem, ssem, wsend, wrecv, ysend, yrecv, xsend, xrecv, csend, crecv, qsend, qrecv,
    msend, mrecv, nsend, nrecv, rsend, rrecv, zsend, zrecv, ksend, krecv, gsend, grecv,
):
    z, y, x, c = place()
    t = x * C + c
    me = y * T + t
    share = act.shape[1]
    k_rows = wk.shape[1]
    features = enc.shape[1]
    weights, sums, rs = (wk, wv), (ksum, vsum), (krs, vrs)
    own, pages, kept = (kown, vown), (kpages, vpages), (kkept, vkept)
    locals_ = []
    sends = []

    def local(src, dst):
        cp = pltpu.make_async_copy(src, dst, lsem.at[len(locals_)])
        cp.start()
        locals_.append(cp)
        return cp

    def go(cp):
        cp.start()
        sends.append(cp)

    def arrived(src, dst, send, recv):
        remote(src, dst, send, recv, z, y, x, 1 - c).wait_recv()

    def zpeer(d, h):
        return (z + h) % Z if d == 0 else (z + Z - h) % Z

    def xpeer(d, h):
        return (x + h) % X if d == 0 else (x + X - h) % X

    def staging(i, slot):
        rows = pl.ds(pl.multiple_of(i * share, share), share)
        return pltpu.make_async_copy(enc.at[rows], staged.at[slot], ssem.at[slot])

    half = k_rows // 2

    def wpart(s, src_z, k):
        return weights[s].at[src_z, pl.ds(k * half, half)]

    def wcopy(d, h, s, k):
        dst = wpart(s, zpeer(1 - d, h - 1), k)
        src = w.at[pl.ds(k * half, half), pl.ds(s * Y * HEAD, Y * HEAD)] if h == 1 else dst
        return remote(src, dst, wsend.at[d, h - 1, s, k], wrecv.at[d, h - 1, s, k], zpeer(d, 1), y, x, c)

    def wbegin(s):
        for k in range(2):
            for d in range(2):
                go(wcopy(d, 1, s, k))

    def wevent(s, h):
        for k in range(2):
            for d in range(2):
                hops = hop_counts(Z, k)[d]
                if h <= hops:
                    dst = wpart(s, zpeer(1 - d, h), k)
                    arrived(dst, dst, wsend.at[d, h - 1, s, k], wrecv.at[d, h - 1, s, k])
                    if h + 1 <= hops:
                        go(wcopy(d, h + 1, s, k))

    def rows_at(k, src_x, core, hf):
        return afull.at[(y + k) % Y, src_x * C + core, pl.ds(hf * (share // 2), share // 2)]

    def xcopy(d, h, k, hf):
        part = rows_at(k, xpeer(1 - d, h - 1), c, hf)
        return remote(part, part, xsend.at[d, h - 1, k, hf], xrecv.at[d, h - 1, k, hf], z, y, xpeer(d, 1), c)

    def ccopy(slot, k, hf):
        part = rows_at(k, (x + X - slot) % X, c, hf)
        return remote(part, part, csend.at[slot, k, hf], crecv.at[slot, k, hf], z, y, x, 1 - c)

    def yevent(k):
        part = afull.at[(y + k) % Y, t]
        arrived(part, part, ysend.at[Y - k], yrecv.at[Y - k])
        for hf in range(2):
            for d in range(2):
                go(xcopy(d, 1, k, hf))
        for hf in range(2):
            go(ccopy(0, k, hf))

    def xevent(h, k):
        for hf in range(2):
            for d in range(2):
                hops = hop_counts(X, hf)[d]
                if h <= hops:
                    part = rows_at(k, xpeer(1 - d, h), c, hf)
                    arrived(part, part, xsend.at[d, h - 1, k, hf], xrecv.at[d, h - 1, k, hf])
                    if h + 1 <= hops:
                        go(xcopy(d, h + 1, k, hf))
                    go(ccopy(h if d == 0 else X - h, k, hf))

    def cevent(j):
        slot = (X - ORIGINS[j]) % X
        for k in (1, 3, 2):
            for hf in range(2):
                part = rows_at(k, (x + ORIGINS[j]) % X, 1 - c, hf)
                arrived(part, part, csend.at[slot, k, hf], crecv.at[slot, k, hf])

    def inverse_of(slot):
        total = jnp.zeros((share, HEAD), jnp.float32)
        for i in range(features // 1024):
            h = staged[slot, :, i * 1024 : (i + 1) * 1024].astype(jnp.float32)
            h = h * h
            for u in range(1024 // HEAD):
                total += h[:, u * HEAD : (u + 1) * HEAD]
        return lax.rsqrt(jnp.sum(total, axis=1, keepdims=True) / features + epsilon)

    def normed(slot, inverse, zz, yy):
        cols = pl.ds(pl.multiple_of((zz * Y + yy) * k_rows, k_rows), k_rows)
        h = staged[slot, :, cols].astype(jnp.float32)
        return (h * inverse * gain[:, cols].astype(jnp.float32)).astype(jnp.bfloat16)

    def norm_own(i):
        slot = i % 2
        staging(i, slot).wait()
        inverse = inverse_of(slot)
        for zz in range(Z):
            afull[y, i, :, zz * k_rows : (zz + 1) * k_rows] = normed(slot, inverse, zz, y)
        if i + 2 < T:
            staging(i + 2, slot).start()

    def chip_of(j):
        return pl.ds(pl.multiple_of(((x + ORIGINS[j]) % X) * C, C), C)

    def project(s, j):
        @pl.loop(0, Y // 2)
        def _(i):
            owners = pl.ds(i * 2, 2)
            rows = afull[owners, chip_of(j)].reshape(2 * C * share, Z * k_rows)
            total = jnp.dot(rows, weights[s][...].reshape(Z * k_rows, Y * HEAD), preferred_element_type=jnp.float32)
            for d in range(Y):
                block = total[:, d * HEAD : (d + 1) * HEAD].reshape(2, C, share, HEAD)
                sums[s][d, owners, chip_of(j)] = block.astype(sums[s].dtype)
                if s == VALUES:
                    @pl.when(y == d)
                    def _():
                        vmine[owners, chip_of(j)] = block

    def reduce_begin(i):
        s, j = ORDER[i]
        for k in (2, 1, 3):
            dst = (y + k) % Y
            go(remote(sums[s].at[dst, :, chip_of(j)], rs[s].at[k - 1, :, chip_of(j)], rsend.at[s, k, j], rrecv.at[s, k, j], z, dst, x, c))

    def zcopy(d, h, s, j):
        dst = pages[s].at[zpeer(1 - d, h - 1), :, chip_of(j)]
        src = own[s].at[:, chip_of(j)] if h == 1 else dst
        return remote(src, dst, zsend.at[d, h - 1, s, j], zrecv.at[d, h - 1, s, j], zpeer(d, 1), y, x, c)

    def finish(i):
        s, j = ORDER[i]
        for k in (1, 3, 2):
            dst = rs[s].at[k - 1, :, chip_of(j)]
            arrived(dst, dst, rsend.at[s, k, j], rrecv.at[s, k, j])
        for m in range(Y):
            total = ksum[y, m, chip_of(j)] if s == KEYS else vmine[m, chip_of(j)]
            for k in range(1, Y):
                total += rs[s][k - 1, m, chip_of(j)].astype(jnp.float32)
            own[s][m, chip_of(j)] = total.astype(own[s].dtype)
        for d in range(2):
            go(zcopy(d, 1, s, j))
        local(own[s].at[:, chip_of(j)], pages[s].at[z, :, chip_of(j)])
        if i + AHEAD < len(ORDER):
            reduce_begin(i + AHEAD)

    def pass_on(h, i):
        s, j = ORDER[i]
        for d in range(2):
            hops = hop_counts(Z, j)[d]
            if h <= hops:
                dst = pages[s].at[zpeer(1 - d, h), :, chip_of(j)]
                arrived(dst, dst, zsend.at[d, h - 1, s, j], zrecv.at[d, h - 1, s, j])
                if h + 1 <= hops:
                    go(zcopy(d, h + 1, s, j))

    pairs = q.shape[0] // 16

    def pages_of(r, pair):
        first = pair * 2 * NBRS
        return [ids[r, 5, first], ids[r, 5, first + 1], ids[r, 5, first + 3]]

    def score(r):
        row = lax.broadcasted_iota(jnp.int32, (NBRS * GROUP, 1), 0)
        second = (row // 8) % 2 == 1

        @pl.loop(0, pairs, unroll=True)
        def _(pair):
            rows_q = qfull[r, :, pl.ds(pair * 16, 16), :].reshape(NBRS * GROUP, HEAD)
            scores = []
            for n, page in enumerate(pages_of(r, pair)):
                keys = kpages[page // 16, (page // 4) % 4, pl.ds((page % 4) * 2, 2)].reshape(2 * share, HEAD)
                s = lax.dot_general(rows_q, keys, (((1,), (1,)), ((), ())), preferred_element_type=jnp.float32)
                s = s * HEAD ** (-0.5)
                ok = mfull[page // 4, pl.ds(1 + page % 4, 1), :] != 0
                if n == 0:
                    ok = jnp.logical_and(ok, jnp.logical_not(second))
                elif n == 2:
                    ok = jnp.logical_and(ok, second)
                scores.append(jnp.where(ok, s, masked_score))
            s = jnp.concatenate(scores, axis=1)
            e = jnp.exp(s - jnp.max(s, axis=1, keepdims=True))
            probs[r, pair] = (e / jnp.sum(e, axis=1, keepdims=True)).astype(jnp.bfloat16)

    def mix(r):
        @pl.loop(0, pairs, unroll=True)
        def _(pair):
            values = [
                vpages[page // 16, (page // 4) % 4, pl.ds((page % 4) * 2, 2)].reshape(2 * share, HEAD)
                for page in pages_of(r, pair)
            ]
            mixed = jnp.dot(probs[r, pair], jnp.concatenate(values, axis=0), preferred_element_type=jnp.float32)
            ctx[r, :, pl.ds(pair * 16, 16), :] = mixed.astype(ctx.dtype).reshape(T, 16, HEAD)

    def head_cols(py, pt):
        return pl.ds(pl.multiple_of((pt * Y + py) * HEAD, HEAD), HEAD)

    def qcopy(k):
        p = (me + k) % (Y * T)
        py, pt = p // T, p % T
        return remote(q.at[:, head_cols(py, pt)], qfull.at[y, t], qsend.at[k], qrecv.at[k], z, py, pt // C, pt % C)

    def gcopy(ky, kt):
        py, pt = (y + ky) % Y, (t + kt) % T
        sem = ky * T + kt
        return remote(ctx.at[py, pt], out.at[:, head_cols(y, t)], gsend.at[sem], grecv.at[sem], z, py, pt // C, pt % C)

    staging(t, 0).start()
    greet_plane([((z + k) % Z, y, x, c) for k in range(1, Z)])
    wbegin(KEYS)
    for s in range(2):
        local(w.at[:, pl.ds(s * Y * HEAD, Y * HEAD)], weights[s].at[z])
    mine_in = local(meta, mfull.at[z * Y + y])

    staging(t, 0).wait()
    inverse = inverse_of(0)
    for yy in range(Y):
        for zz in range(Z):
            act[yy, :, zz * k_rows : (zz + 1) * k_rows] = normed(0, inverse, zz, yy)
    for k in (1, 3, 2):
        dst = (y + k) % Y
        go(remote(act.at[dst], afull.at[y, t], ysend.at[k], yrecv.at[k], z, dst, x, c))
    for k in (1, 3, 2):
        go(remote(meta, mfull.at[z * Y + y], msend.at[k], mrecv.at[k], z, (y + k) % Y, x, c))
    for i in range(2):
        staging(i, i).start()

    wevent(KEYS, 1)
    norm_own(0)
    norm_own(1)
    wevent(KEYS, 2)
    yevent(1)
    yevent(3)
    norm_own(2)
    norm_own(3)
    yevent(2)
    wevent(KEYS, 3)
    wbegin(VALUES)
    xevent(1, 1)
    norm_own(4)
    norm_own(5)
    xevent(1, 3)
    norm_own(6)
    norm_own(7)
    wevent(KEYS, 4)
    locals_[0].wait()
    locals_[1].wait()
    cevent(0)
    project(KEYS, 0)
    reduce_begin(0)
    wevent(VALUES, 1)
    xevent(1, 2)
    wevent(VALUES, 2)
    cevent(1)
    project(KEYS, 1)
    reduce_begin(1)
    xevent(2, 1)
    cevent(2)
    project(KEYS, 2)
    wevent(VALUES, 3)
    xevent(2, 3)
    finish(0)
    wevent(VALUES, 4)
    xevent(2, 2)

    mine_in.wait()
    for k in (1, 3, 2):
        theirs = mfull.at[z * Y + (y + k) % Y]
        arrived(theirs, theirs, msend.at[Y - k], mrecv.at[Y - k])
    for k in range(1, Z):
        mine = mfull.at[pl.ds(z * Y, Y)]
        go(remote(mine, mine, nsend.at[k], nrecv.at[k], (z + k) % Z, y, x, c))

    pass_on(1, 0)
    cevent(3)
    project(KEYS, 3)
    finish(1)
    pass_on(2, 0)
    project(VALUES, 0)
    project(VALUES, 1)
    pass_on(1, 1)
    project(VALUES, 2)
    pass_on(3, 0)
    project(VALUES, 3)

    @pl.loop(1, Y * T)
    def _(k):
        qcopy(k).start()

    local(q.at[:, head_cols(y, t)], qfull.at[y, t])
    pass_on(4, 0)
    pass_on(2, 1)

    work = []
    for i in range(2, len(ORDER) + 1):
        if i < len(ORDER):
            finish(i)
        pass_on(3, i - 1)
        if i < len(ORDER):
            pass_on(1, i)
        if work:
            work.pop(0)()
        pass_on(4, i - 1)
        if i < len(ORDER):
            pass_on(2, i)
        if i == X:
            for k in range(1, Z):
                theirs = mfull.at[pl.ds(((z + Z - k) % Z) * Y, Y)]
                arrived(theirs, theirs, nsend.at[k], nrecv.at[k])
            facts = local(mfull.at[pl.ds(z * Y, Y)], ids)
            local(mfull, mout)

            @pl.loop(1, Y * T)
            def _(k):
                p = (me + Y * T - k) % (Y * T)
                part = qfull.at[p // T, p % T]
                arrived(part, part, qsend.at[k], qrecv.at[k])

            for cp in locals_[3:]:
                cp.wait()
            waited = len(locals_)
            work = [functools.partial(score, r) for r in range(Y)]
        if i == len(ORDER) - 1:
            for s in range(2):
                for k in range(1, Y):
                    m = (y + k) % Y
                    go(remote(own[s].at[m], kept[s].at[y], ksend.at[s, k], krecv.at[s, k], z, m, x, c))
                local(own[s].at[y], kept[s].at[y])
    while work:
        work.pop(0)()
    for cp in locals_[waited:]:
        cp.wait()

    for ky in (2, 1, 3, 0):
        mix((y + ky) % Y)

        @pl.loop(0 if ky else 1, T)
        def _(kt):
            gcopy(ky, kt).start()

    last = pltpu.make_async_copy(ctx.at[y, t], out.at[:, head_cols(y, t)], lsem.at[len(locals_)])
    last.start()
    for s in range(2):
        for k in range(1, Y):
            part = kept[s].at[(y + Y - k) % Y]
            arrived(part, part, ksend.at[s, k], krecv.at[s, k])
    for cp in sends:
        cp.wait_send()

    @pl.loop(1, Y * T)
    def _(k):
        qcopy(k).wait_send()

    for ky in (2, 1, 3, 0):
        @pl.loop(0 if ky else 1, T)
        def _(kt):
            sem = ky * T + kt
            cols = head_cols((y + Y - ky) % Y, (t + T - kt) % T)
            arrived(ctx.at[y, t], out.at[:, cols], gsend.at[sem], grecv.at[sem])
            gcopy(ky, kt).wait_send()

    last.wait()


def layer(enc, gain, w, q, meta):
    dma = pltpu.SemaphoreType.DMA
    bf16, f32 = jnp.bfloat16, jnp.float32
    share = enc.shape[0] // T
    k_rows = w.shape[0]
    depth = Z * k_rows
    block = (Y, T, share, HEAD)
    hbm = pl.BlockSpec(memory_space=pl.ANY)
    kept = jax.ShapeDtypeStruct(block, bf16)
    pairs = q.shape[0] // 16
    return pl.pallas_call(
        layer_kernel,
        out_shape=(
            jax.ShapeDtypeStruct(q.shape, bf16),
            kept,
            kept,
            jax.ShapeDtypeStruct((Z * Y,) + meta.shape, meta.dtype),
        ),
        in_specs=[hbm, pl.BlockSpec(memory_space=pltpu.VMEM), hbm, hbm, hbm],
        out_specs=[hbm] * 4,
        scratch_shapes=[
            pltpu.VMEM((2, share, enc.shape[1]), bf16),
            pltpu.VMEM((Y, share, depth), bf16),
            pltpu.VMEM((Y, T, share, depth), bf16),
            pltpu.VMEM((Z, k_rows, Y * HEAD), bf16),
            pltpu.VMEM((Z, k_rows, Y * HEAD), bf16),
            pltpu.VMEM((Y,) + block, f32),
            pltpu.VMEM((Y,) + block, bf16),
            pltpu.VMEM(block, f32),
            pltpu.VMEM((Y - 1,) + block, f32),
            pltpu.VMEM((Y - 1,) + block, bf16),
            pltpu.VMEM(block, bf16),
            pltpu.VMEM(block, bf16),
            pltpu.VMEM((Z,) + block, bf16),
            pltpu.VMEM((Z,) + block, bf16),
            pltpu.VMEM((Y, T, q.shape[0], HEAD), bf16),
            pltpu.VMEM((Y, pairs, NBRS * GROUP, 3 * HEAD), bf16),
            pltpu.VMEM((Y, T, q.shape[0], HEAD), bf16),
            pltpu.VMEM((Z * Y,) + meta.shape, meta.dtype),
            pltpu.SMEM((Y,) + meta.shape, meta.dtype),
            dma((24,)),
            dma((2,)),
            dma((2, Z // 2, 2, 2)), dma((2, Z // 2, 2, 2)),
            dma((Y,)), dma((Y,)),
            dma((2, X // 2, Y, 2)), dma((2, X // 2, Y, 2)),
            dma((X, Y, 2)), dma((X, Y, 2)),
            dma((Y * T,)), dma((Y * T,)),
            dma((Y,)), dma((Y,)),
            dma((Z,)), dma((Z,)),
            dma((2, Y, X)), dma((2, Y, X)),
            dma((2, Z // 2, 2, X)), dma((2, Z // 2, 2, X)),
            dma((2, Y)), dma((2, Y)),
            dma((Y * T,)), dma((Y * T,)),
        ],
        compiler_params=pltpu.CompilerParams(
            has_side_effects=True, collective_id=1, vmem_limit_bytes=60 * 2**20
        ),
        name="layer",
    )(enc, gain, w, q, meta)


def shards(
    queries, enc_hidden, enc_gain, kv_weight, neighbour_pages, reader_counts, neighbour_tokens
):
    dp = lax.axis_index("dp")
    z, y = dp // Y, dp % Y
    t = lax.axis_index("tensor")
    pages_here, nb_tokens, features = enc_hidden.shape
    groups_here = queries.shape[0]
    k_rows = kv_weight.shape[0]
    rows_here = pages_here * nb_tokens
    w = kv_weight.reshape(k_rows, -1)

    facts = jnp.concatenate(
        [
            reader_counts,
            neighbour_tokens,
            jnp.pad(neighbour_pages.reshape(1, -1), ((0, 2), (0, nb_tokens - groups_here * NBRS))),
        ]
    )
    context, kkept, vkept, mfull = layer(
        enc_hidden.reshape(rows_here, features),
        enc_gain.reshape(1, features),
        w,
        queries.reshape(-1, queries.shape[2]),
        facts,
    )
    context = context.reshape(queries.shape)

    totals = lax.dynamic_slice_in_dim(jnp.sum(mfull[:, 0], axis=0), dp * pages_here, pages_here, 0)
    kept = jnp.stack([kkept, vkept]).reshape(2, Y, pages_here, nb_tokens, HEAD).transpose(2, 3, 0, 1, 4)
    kept = kept.reshape(pages_here, nb_tokens, 2, Y * HEAD)
    kept_pages = jnp.where((totals > 0)[:, None, None, None], kept, jnp.zeros_like(kept))
    return (context, kept_pages)


def solution(mesh):
    placed = (
        P("dp", "tensor", None),
        P("dp", None, None),
        P(),
        P("dp", None, "tensor"),
        P("dp", None),
        P("dp", None),
        P("dp", None),
    )
    return jax.shard_map(
        shards,
        mesh=mesh,
        in_specs=placed,
        out_specs=(P("dp", "tensor", None), P("dp", None, None, "tensor")),
        check_vma=False,
    )
```

```python
import functools

import jax
import jax.numpy as jnp
from jax import lax
from jax.experimental import pallas as pl
from jax.experimental.pallas import tpu as pltpu
from jax.sharding import PartitionSpec as P

HEAD = 128
GROUP = 64
NBRS = 2
Z, Y, X, C = 8, 4, 4, 2
T = X * C
MESH = pl.DeviceIdType.MESH

epsilon = 1e-05
masked_score = -1e30


def place():
    dp = lax.axis_index("dp")
    t = lax.axis_index("tensor")
    return dp // Y, dp % Y, t // C, t % C


def remote(src, dst, send, recv, z, y, x, c):
    return pltpu.make_async_remote_copy(
        src_ref=src,
        dst_ref=dst,
        send_sem=send,
        recv_sem=recv,
        device_id=(z * Y + y, x * C + c),
        device_id_type=MESH,
    )


def greet_plane(also=()):
    z, y, x, c = place()
    me = y * T + x * C + c
    barrier = pltpu.get_barrier_semaphore()

    @pl.loop(1, Y * T)
    def _(k):
        p = (me + k) % (Y * T)
        pl.semaphore_signal(barrier, inc=1, device_id=(z * Y + p // T, p % T), device_id_type=MESH)

    for pz, py, px, pc in also:
        pl.semaphore_signal(barrier, inc=1, device_id=(pz * Y + py, px * C + pc), device_id_type=MESH)
    pl.semaphore_wait(barrier, Y * T - 1 + len(also))


def hop_counts(n, c):
    far, near = n // 2, n - 1 - n // 2
    return (far, near) if c % 2 == 0 else (near, far)


KEYS, VALUES = 0, 1
ORIGINS = (0, 1, 3, 2)
ORDER = [(VALUES, j) for j in range(X - 1)] + [(KEYS, j) for j in range(X)] + [(VALUES, X - 1)]
KEYS_DONE = 6
WINDOW = 2


def layer_kernel(
    enc, gain, w, q, meta, out, kkept, vkept,
    gain32, staged, act, afull, wk, wv, ksum, vsum, vmine, krs, vrs, kown, vown, kpages, vpages,
    qfull, probs, ctx, mfull, ids, kmask, vmask,
    lsem, ssem, wsend, wrecv, ysend, yrecv, xsend, xrecv, csend, crecv, qsend, qrecv,
    msend, mrecv, nsend, nrecv, rsend, rrecv, zsend, zrecv, ksend, krecv, gsend, grecv,
):
    z, y, x, c = place()
    t = x * C + c
    me = y * T + t
    share = act.shape[1]
    k_rows = wk.shape[1]
    features = enc.shape[1]
    weights, sums, rs = (wk, wv), (ksum, vsum), (krs, vrs)
    own, pages, kept = (kown, vown), (kpages, vpages), (kkept, vkept)
    locals_ = []
    sends = []

    def local(src, dst):
        cp = pltpu.make_async_copy(src, dst, lsem.at[len(locals_)])
        cp.start()
        locals_.append(cp)
        return cp

    def go(cp):
        cp.start()
        sends.append(cp)

    def arrived(src, dst, send, recv):
        remote(src, dst, send, recv, z, y, x, 1 - c).wait_recv()

    def zpeer(d, h):
        return (z + h) % Z if d == 0 else (z + Z - h) % Z

    def xpeer(d, h):
        return (x + h) % X if d == 0 else (x + X - h) % X

    def staging(i, slot):
        rows = pl.ds(pl.multiple_of(i * share, share), share)
        return pltpu.make_async_copy(enc.at[rows], staged.at[slot], ssem.at[slot])

    half = k_rows // 2

    def wpart(s, src_z, k):
        return weights[s].at[src_z, pl.ds(k * half, half)]

    def wcopy(d, h, s, k):
        dst = wpart(s, zpeer(1 - d, h - 1), k)
        src = w.at[pl.ds(k * half, half), pl.ds(s * Y * HEAD, Y * HEAD)] if h == 1 else dst
        return remote(src, dst, wsend.at[d, h - 1, s, k], wrecv.at[d, h - 1, s, k], zpeer(d, 1), y, x, c)

    def wbegin(s):
        for k in range(2):
            for d in range(2):
                go(wcopy(d, 1, s, k))

    def wevent(s, h):
        for k in range(2):
            for d in range(2):
                hops = hop_counts(Z, k)[d]
                if h <= hops:
                    dst = wpart(s, zpeer(1 - d, h), k)
                    arrived(dst, dst, wsend.at[d, h - 1, s, k], wrecv.at[d, h - 1, s, k])
                    if h + 1 <= hops:
                        go(wcopy(d, h + 1, s, k))

    def rows_at(k, src_x, core, hf):
        return afull.at[(y + k) % Y, src_x * C + core, pl.ds(hf * (share // 2), share // 2)]

    def xcopy(d, h, k, hf):
        part = rows_at(k, xpeer(1 - d, h - 1), c, hf)
        return remote(part, part, xsend.at[d, h - 1, k, hf], xrecv.at[d, h - 1, k, hf], z, y, xpeer(d, 1), c)

    def ccopy(slot, k, hf):
        part = rows_at(k, (x + X - slot) % X, c, hf)
        return remote(part, part, csend.at[slot, k, hf], crecv.at[slot, k, hf], z, y, x, 1 - c)

    def yevent(k):
        part = afull.at[(y + k) % Y, t]
        arrived(part, part, ysend.at[Y - k], yrecv.at[Y - k])
        for hf in range(2):
            for d in range(2):
                go(xcopy(d, 1, k, hf))
        for hf in range(2):
            go(ccopy(0, k, hf))

    def xevent(h, k):
        for hf in range(2):
            for d in range(2):
                hops = hop_counts(X, hf)[d]
                if h <= hops:
                    part = rows_at(k, xpeer(1 - d, h), c, hf)
                    arrived(part, part, xsend.at[d, h - 1, k, hf], xrecv.at[d, h - 1, k, hf])
                    if h + 1 <= hops:
                        go(xcopy(d, h + 1, k, hf))
                    go(ccopy(h if d == 0 else X - h, k, hf))

    def cevent(j):
        slot = (X - ORIGINS[j]) % X
        for k in (1, 3, 2):
            for hf in range(2):
                part = rows_at(k, (x + ORIGINS[j]) % X, 1 - c, hf)
                arrived(part, part, csend.at[slot, k, hf], crecv.at[slot, k, hf])

    def inverse_of(slot):
        total = jnp.zeros((share, HEAD), jnp.float32)
        for i in range(features // 1024):
            h = staged[slot, :, i * 1024 : (i + 1) * 1024].astype(jnp.float32)
            h = h * h
            for u in range(1024 // HEAD):
                total += h[:, u * HEAD : (u + 1) * HEAD]
        return lax.rsqrt(jnp.sum(total, axis=1, keepdims=True) / features + epsilon)

    def normed(slot, inverse, zz, yy):
        parts = []
        for u in range(k_rows // HEAD):
            col = (zz * Y + yy) * (k_rows // HEAD) + u
            h = staged[slot, :, pl.ds(pl.multiple_of(col * HEAD, HEAD), HEAD)].astype(jnp.float32)
            parts.append((h * inverse * gain32[pl.ds(col, 1), :]).astype(jnp.bfloat16))
        return jnp.concatenate(parts, axis=1)

    def norm_own(i):
        slot = i % 2
        staging(i, slot).wait()
        inverse = inverse_of(slot)
        for zz in range(Z):
            afull[y, i, :, zz * k_rows : (zz + 1) * k_rows] = normed(slot, inverse, zz, y)
        if i + 2 < T:
            staging(i + 2, slot).start()

    def chip_of(j):
        return pl.ds(pl.multiple_of(((x + ORIGINS[j]) % X) * C, C), C)

    def project(s, j):
        @pl.loop(0, Y // 2)
        def _(i):
            owners = pl.ds(i * 2, 2)
            rows = afull[owners, chip_of(j)].reshape(2 * C * share, Z * k_rows)
            total = jnp.dot(rows, weights[s][...].reshape(Z * k_rows, Y * HEAD), preferred_element_type=jnp.float32)
            for d in range(Y):
                block = total[:, d * HEAD : (d + 1) * HEAD].reshape(2, C, share, HEAD)
                sums[s][d, owners, chip_of(j)] = block.astype(sums[s].dtype)
                if s == VALUES:
                    @pl.when(y == d)
                    def _():
                        vmine[owners, chip_of(j)] = block

    def reduce_begin(i):
        s, j = ORDER[i]
        for k in (2, 1, 3):
            dst = (y + k) % Y
            go(remote(sums[s].at[dst, :, chip_of(j)], rs[s].at[k - 1, :, chip_of(j)], rsend.at[s, k, j], rrecv.at[s, k, j], z, dst, x, c))

    def zcopy(d, h, s, j):
        dst = pages[s].at[zpeer(1 - d, h - 1), :, chip_of(j)]
        src = own[s].at[:, chip_of(j)] if h == 1 else dst
        return remote(src, dst, zsend.at[d, h - 1, s, j], zrecv.at[d, h - 1, s, j], zpeer(d, 1), y, x, c)

    def finish(i):
        s, j = ORDER[i]
        for k in (1, 3, 2):
            dst = rs[s].at[k - 1, :, chip_of(j)]
            arrived(dst, dst, rsend.at[s, k, j], rrecv.at[s, k, j])
        for m in range(Y):
            total = ksum[y, m, chip_of(j)] if s == KEYS else vmine[m, chip_of(j)]
            for k in range(1, Y):
                total += rs[s][k - 1, m, chip_of(j)].astype(jnp.float32)
            own[s][m, chip_of(j)] = total.astype(own[s].dtype)
        for d in range(2):
            go(zcopy(d, 1, s, j))
        local(own[s].at[:, chip_of(j)], pages[s].at[z, :, chip_of(j)])

    def pass_on(h, i):
        s, j = ORDER[i]
        for d in range(2):
            hops = hop_counts(Z, j)[d]
            if h <= hops:
                dst = pages[s].at[zpeer(1 - d, h), :, chip_of(j)]
                arrived(dst, dst, zsend.at[d, h - 1, s, j], zrecv.at[d, h - 1, s, j])
                if h + 1 <= hops:
                    go(zcopy(d, h + 1, s, j))

    pairs = q.shape[0] // 16

    def pages_of(r, pair):
        return [ids[r, 5, pair * 2], ids[r, 6, pair * 2], ids[r, 6, pair * 2 + 1]]

    def score(r):
        row = lax.broadcasted_iota(jnp.int32, (NBRS * GROUP, 1), 0)
        second = (row // 8) % 2 == 1

        @pl.loop(0, pairs, unroll=True)
        def _(pair):
            rows_q = qfull[r, :, pl.ds(pair * 16, 16), :].reshape(NBRS * GROUP, HEAD)
            scores = []
            for n, page in enumerate(pages_of(r, pair)):
                keys = kpages[page // 16, (page // 4) % 4, pl.ds((page % 4) * 2, 2)].reshape(2 * share, HEAD)
                s = lax.dot_general(rows_q, keys, (((1,), (1,)), ((), ())), preferred_element_type=jnp.float32)
                s = s * HEAD ** (-0.5)
                ok = mfull[page // 4, pl.ds(1 + page % 4, 1), :] != 0
                if n == 0:
                    ok = jnp.logical_and(ok, jnp.logical_not(second))
                elif n == 2:
                    ok = jnp.logical_and(ok, second)
                scores.append(jnp.where(ok, s, masked_score))
            s = jnp.concatenate(scores, axis=1)
            e = jnp.exp(s - jnp.max(s, axis=1, keepdims=True))
            probs[r, pair] = (e / jnp.sum(e, axis=1, keepdims=True)).astype(jnp.bfloat16)

    def mix(r):
        @pl.loop(0, pairs, unroll=True)
        def _(pair):
            values = [
                vpages[page // 16, (page // 4) % 4, pl.ds((page % 4) * 2, 2)].reshape(2 * share, HEAD)
                for page in pages_of(r, pair)
            ]
            mixed = jnp.dot(probs[r, pair], jnp.concatenate(values, axis=0), preferred_element_type=jnp.float32)
            ctx[r, :, pl.ds(pair * 16, 16), :] = mixed.astype(ctx.dtype).reshape(T, 16, HEAD)

    def head_cols(py, pt):
        return pl.ds(pl.multiple_of((pt * Y + py) * HEAD, HEAD), HEAD)

    def qcopy(k):
        p = (me + k) % (Y * T)
        py, pt = p // T, p % T
        return remote(q.at[:, head_cols(py, pt)], qfull.at[y, t], qsend.at[k], qrecv.at[k], z, py, pt // C, pt % C)

    def gcopy(ky, kt):
        py, pt = (y + ky) % Y, (t + kt) % T
        sem = ky * T + kt
        return remote(ctx.at[py, pt], out.at[:, head_cols(y, t)], gsend.at[sem], grecv.at[sem], z, py, pt // C, pt % C)

    def keep():
        totals = jnp.sum(mfull[:, 0, :], axis=0, keepdims=True)
        lane = lax.broadcasted_iota(jnp.int32, (1, meta.shape[1]), 1)
        slots = Y
        span = T // slots
        for m in range(Y):
            for slot in range(slots):
                at = pl.ds(slot * span, span)
                reads = jnp.sum(jnp.where(lane == (z * Y + m) * slots + slot, totals, 0), axis=1, keepdims=True)
                for s, masked in enumerate((kmask, vmask)):
                    rows = own[s][m, at].reshape(span * share, HEAD)
                    rows = jnp.where(reads > 0, rows, jnp.zeros_like(rows))
                    masked[m, slot * span * share : (slot + 1) * span * share] = rows
        for s, masked in enumerate((kmask, vmask)):
            for k in (2, 1, 3):
                m = (y + k) % Y
                go(remote(masked.at[m], kept[s].at[y], ksend.at[s, k], krecv.at[s, k], z, m, x, c))
            local(masked.at[y], kept[s].at[y])

    def ask():
        @pl.loop(1, Y * T)
        def _(k):
            qcopy(k).start()

        local(q.at[:, head_cols(y, t)], qfull.at[y, t])

    def tell():
        for k in (1, 3, 2):
            theirs = mfull.at[z * Y + (y + k) % Y]
            arrived(theirs, theirs, msend.at[Y - k], mrecv.at[Y - k])
        for k in range(1, Z):
            mine = mfull.at[pl.ds(z * Y, Y)]
            go(remote(mine, mine, nsend.at[k], nrecv.at[k], (z + k) % Z, y, x, c))

    def hear():
        for k in range(1, Z):
            theirs = mfull.at[pl.ds(((z + Z - k) % Z) * Y, Y)]
            arrived(theirs, theirs, nsend.at[k], nrecv.at[k])

    def told():
        local(mfull.at[pl.ds(z * Y, Y)], ids)

        @pl.loop(1, Y * T)
        def _(k):
            p = (me + Y * T - k) % (Y * T)
            part = qfull.at[p // T, p % T]
            arrived(part, part, qsend.at[k], qrecv.at[k])

    def settle():
        for cp in locals_[len(settled):]:
            cp.wait()
            settled.append(cp)

    settled = []

    staging(t, 0).start()
    greet_plane([((z + k) % Z, y, x, c) for k in range(1, Z)])
    wbegin(VALUES)
    for s in range(2):
        local(w.at[:, pl.ds(s * Y * HEAD, Y * HEAD)], weights[s].at[z])
    local(meta, mfull.at[z * Y + y])

    gain32[...] = gain[...].astype(jnp.float32)
    staging(t, 0).wait()
    inverse = inverse_of(0)
    for yy in range(Y):
        for zz in range(Z):
            act[yy, :, zz * k_rows : (zz + 1) * k_rows] = normed(0, inverse, zz, yy)
    for k in (1, 3, 2):
        dst = (y + k) % Y
        go(remote(act.at[dst], afull.at[y, t], ysend.at[k], yrecv.at[k], z, dst, x, c))
    for k in (1, 3, 2):
        go(remote(meta, mfull.at[z * Y + y], msend.at[k], mrecv.at[k], z, (y + k) % Y, x, c))
    for i in range(2):
        staging(i, i).start()

    w_, n_, x_, c_, p_ = wevent, norm_own, xevent, cevent, project
    start = [
        (w_, VALUES, 1), (n_, 0), (n_, 1), (yevent, 1), (yevent, 3), (w_, VALUES, 2),
        (n_, 2), (n_, 3), (yevent, 2), (n_, 4), (w_, VALUES, 3), (wbegin, KEYS), (x_, 1, 1), (n_, 5), (n_, 6), (n_, 7),
        (w_, VALUES, 4), (settle,), (c_, 0), (p_, VALUES, 0), (reduce_begin, 0), (ask,),
        (x_, 1, 3), (w_, KEYS, 1), (x_, 1, 2), (c_, 1), (p_, VALUES, 1), (reduce_begin, 1),
        (w_, KEYS, 2), (c_, 2), (p_, VALUES, 2), (finish, 0), (reduce_begin, 2),
        (w_, KEYS, 3), (x_, 2, 1), (finish, 1), (pass_on, 1, 0), (w_, KEYS, 4), (p_, KEYS, 0), (reduce_begin, 3),
        (x_, 2, 3), (pass_on, 1, 1), (pass_on, 2, 0), (x_, 2, 2), (p_, KEYS, 1), (finish, 2), (reduce_begin, 4),
        (pass_on, 2, 1), (pass_on, 3, 0), (c_, 3), (tell,), (p_, KEYS, 2),
    ]
    for f, *rest in start:
        f(*rest)
    work = [(project, KEYS, 3), (project, VALUES, 3)]
    n = len(ORDER)
    begun = 5
    done = {(1, 0), (2, 0), (1, 1), (2, 1), (3, 0)}
    for i in range(3, n + 4):
        if i < n:
            finish(i)
            while begun < min(n, i + 1 + WINDOW):
                reduce_begin(begun)
                begun += 1
        for h in (4, 3, 2, 1):
            k = i - h
            if 0 <= k < n and (h, k) not in done:
                pass_on(h, k)
                done.add((h, k))
            if work and (h == 3 or k > KEYS_DONE):
                f, *rest = work.pop(0)
                f(*rest)
            if (h, k) == (4, KEYS_DONE):
                told()
                settle()
                work += [(score, r) for r in range(Y)]
            if (h, k) == (1, n - 1):
                hear()
                keep()
    for f, *rest in work:
        f(*rest)
    settle()

    for ky in (2, 1, 3, 0):
        mix((y + ky) % Y)

        @pl.loop(0 if ky else 1, T)
        def _(kt):
            gcopy(ky, kt).start()

    last = pltpu.make_async_copy(ctx.at[y, t], out.at[:, head_cols(y, t)], lsem.at[len(locals_)])
    last.start()
    for s in range(2):
        for k in range(1, Y):
            part = kept[s].at[(y + Y - k) % Y]
            arrived(part, part, ksend.at[s, k], krecv.at[s, k])
    for cp in sends:
        cp.wait_send()

    @pl.loop(1, Y * T)
    def _(k):
        qcopy(k).wait_send()

    for ky in (2, 1, 3, 0):
        @pl.loop(0 if ky else 1, T)
        def _(kt):
            sem = ky * T + kt
            cols = head_cols((y + Y - ky) % Y, (t + T - kt) % T)
            arrived(ctx.at[y, t], out.at[:, cols], gsend.at[sem], grecv.at[sem])
            gcopy(ky, kt).wait_send()

    last.wait()
    settle()


def layer(enc, gain, w, q, meta):
    dma = pltpu.SemaphoreType.DMA
    bf16, f32 = jnp.bfloat16, jnp.float32
    share = enc.shape[0] // T
    k_rows = w.shape[0]
    depth = Z * k_rows
    block = (Y, T, share, HEAD)
    hbm = pl.BlockSpec(memory_space=pl.ANY)
    kept = jax.ShapeDtypeStruct((Y, T * share, HEAD), bf16)
    pairs = q.shape[0] // 16
    return pl.pallas_call(
        layer_kernel,
        out_shape=(
            jax.ShapeDtypeStruct(q.shape, bf16),
            kept,
            kept,
        ),
        in_specs=[hbm, pl.BlockSpec(memory_space=pltpu.VMEM), hbm, hbm, hbm],
        out_specs=[hbm] * 3,
        scratch_shapes=[
            pltpu.VMEM(gain.shape, f32),
            pltpu.VMEM((2, share, enc.shape[1]), bf16),
            pltpu.VMEM((Y, share, depth), bf16),
            pltpu.VMEM((Y, T, share, depth), bf16),
            pltpu.VMEM((Z, k_rows, Y * HEAD), bf16),
            pltpu.VMEM((Z, k_rows, Y * HEAD), bf16),
            pltpu.VMEM((Y,) + block, f32),
            pltpu.VMEM((Y,) + block, bf16),
            pltpu.VMEM(block, f32),
            pltpu.VMEM((Y - 1,) + block, f32),
            pltpu.VMEM((Y - 1,) + block, bf16),
            pltpu.VMEM(block, bf16),
            pltpu.VMEM(block, bf16),
            pltpu.VMEM((Z,) + block, bf16),
            pltpu.VMEM((Z,) + block, bf16),
            pltpu.VMEM((Y, T, q.shape[0], HEAD), bf16),
            pltpu.VMEM((Y, pairs, NBRS * GROUP, 3 * HEAD), bf16),
            pltpu.VMEM((Y, T, q.shape[0], HEAD), bf16),
            pltpu.VMEM((Z * Y,) + meta.shape, meta.dtype),
            pltpu.SMEM((Y,) + meta.shape, meta.dtype),
            pltpu.VMEM((Y, T * share, HEAD), bf16),
            pltpu.VMEM((Y, T * share, HEAD), bf16),
            dma((24,)),
            dma((2,)),
            dma((2, Z // 2, 2, 2)), dma((2, Z // 2, 2, 2)),
            dma((Y,)), dma((Y,)),
            dma((2, X // 2, Y, 2)), dma((2, X // 2, Y, 2)),
            dma((X, Y, 2)), dma((X, Y, 2)),
            dma((Y * T,)), dma((Y * T,)),
            dma((Y,)), dma((Y,)),
            dma((Z,)), dma((Z,)),
            dma((2, Y, X)), dma((2, Y, X)),
            dma((2, Z // 2, 2, X)), dma((2, Z // 2, 2, X)),
            dma((2, Y)), dma((2, Y)),
            dma((Y * T,)), dma((Y * T,)),
        ],
        compiler_params=pltpu.CompilerParams(
            has_side_effects=True, collective_id=1, vmem_limit_bytes=60 * 2**20
        ),
        name="layer",
    )(enc, gain, w, q, meta)


def shards(
    queries, enc_hidden, enc_gain, kv_weight, neighbour_pages, reader_counts, neighbour_tokens
):
    pages_here, nb_tokens, features = enc_hidden.shape
    groups_here = queries.shape[0]
    k_rows = kv_weight.shape[0]
    rows_here = pages_here * nb_tokens
    w = kv_weight.reshape(k_rows, -1)

    ids = neighbour_pages.T
    facts = jnp.concatenate(
        [reader_counts, neighbour_tokens, jnp.pad(ids, ((0, 1), (0, nb_tokens - groups_here)))]
    )
    context, kkept, vkept = layer(
        enc_hidden.reshape(rows_here, features),
        enc_gain.reshape(-1, HEAD),
        w,
        queries.reshape(-1, queries.shape[2]),
        facts,
    )
    kept = jnp.stack([kkept, vkept]).reshape(2, Y, pages_here, nb_tokens, HEAD).transpose(2, 3, 0, 1, 4)
    kept_pages = kept.reshape(pages_here, nb_tokens, 2, Y * HEAD)
    return (context.reshape(queries.shape), kept_pages)


def solution(mesh):
    placed = (
        P("dp", "tensor", None),
        P("dp", None, None),
        P(),
        P("dp", None, "tensor"),
        P("dp", None),
        P("dp", None),
        P("dp", None),
    )
    return jax.shard_map(
        shards,
        mesh=mesh,
        in_specs=placed,
        out_specs=(P("dp", "tensor", None), P("dp", None, None, "tensor")),
        check_vma=False,
    )
```

```python
import functools

import jax
import jax.numpy as jnp
from jax import lax
from jax.experimental import pallas as pl
from jax.experimental.pallas import tpu as pltpu
from jax.sharding import PartitionSpec as P

HEAD = 128
GROUP = 64
NBRS = 2
Z, Y, X, C = 8, 4, 4, 2
T = X * C
MESH = pl.DeviceIdType.MESH

epsilon = 1e-05
masked_score = -1e30


def place():
    dp = lax.axis_index("dp")
    t = lax.axis_index("tensor")
    return dp // Y, dp % Y, t // C, t % C


def remote(src, dst, send, recv, z, y, x, c):
    return pltpu.make_async_remote_copy(
        src_ref=src,
        dst_ref=dst,
        send_sem=send,
        recv_sem=recv,
        device_id=(z * Y + y, x * C + c),
        device_id_type=MESH,
    )


def greet_plane(also=()):
    z, y, x, c = place()
    me = y * T + x * C + c
    barrier = pltpu.get_barrier_semaphore()

    @pl.loop(1, Y * T)
    def _(k):
        p = (me + k) % (Y * T)
        pl.semaphore_signal(barrier, inc=1, device_id=(z * Y + p // T, p % T), device_id_type=MESH)

    for pz, py, px, pc in also:
        pl.semaphore_signal(barrier, inc=1, device_id=(pz * Y + py, px * C + pc), device_id_type=MESH)
    pl.semaphore_wait(barrier, Y * T - 1 + len(also))


def hop_counts(n, c):
    far, near = n // 2, n - 1 - n // 2
    return (far, near) if c % 2 == 0 else (near, far)


KEYS, VALUES = 0, 1
ORIGINS = (0, 1, 3, 2)
ORDER = [(VALUES, j) for j in range(X - 1)] + [(KEYS, j) for j in range(X)] + [(VALUES, X - 1)]
KEYS_DONE = 6
WINDOW = 2


def layer_kernel(
    enc, gain, w, q, meta, out, kkept, vkept,
    gain32, staged, act, afull, wk, wv, ksum, vsum, vmine, krs, vrs, kown, vown, kpages, vpages,
    qfull, probs, ctx, mfull, ids, kmask, vmask,
    lsem, ssem, wsend, wrecv, ysend, yrecv, xsend, xrecv, csend, crecv, qsend, qrecv,
    msend, mrecv, nsend, nrecv, rsend, rrecv, zsend, zrecv, ksend, krecv, gsend, grecv,
):
    z, y, x, c = place()
    t = x * C + c
    me = y * T + t
    share = act.shape[1]
    k_rows = wk.shape[1]
    features = enc.shape[1]
    weights, sums, rs = (wk, wv), (ksum, vsum), (krs, vrs)
    own, pages, kept = (kown, vown), (kpages, vpages), (kkept, vkept)
    locals_ = []
    sends = []

    def local(src, dst):
        cp = pltpu.make_async_copy(src, dst, lsem.at[len(locals_)])
        cp.start()
        locals_.append(cp)
        return cp

    def go(cp):
        cp.start()
        sends.append(cp)

    def arrived(src, dst, send, recv):
        remote(src, dst, send, recv, z, y, x, 1 - c).wait_recv()

    def zpeer(d, h):
        return (z + h) % Z if d == 0 else (z + Z - h) % Z

    def xpeer(d, h):
        return (x + h) % X if d == 0 else (x + X - h) % X

    def staging(i, slot):
        rows = pl.ds(pl.multiple_of(i * share, share), share)
        return pltpu.make_async_copy(enc.at[rows], staged.at[slot], ssem.at[slot])

    half = k_rows // 2

    def wpart(s, src_z, k):
        return weights[s].at[src_z, pl.ds(k * half, half)]

    def wcopy(d, h, s, k):
        dst = wpart(s, zpeer(1 - d, h - 1), k)
        src = w.at[pl.ds(k * half, half), pl.ds(s * Y * HEAD, Y * HEAD)] if h == 1 else dst
        return remote(src, dst, wsend.at[d, h - 1, s, k], wrecv.at[d, h - 1, s, k], zpeer(d, 1), y, x, c)

    def wbegin(s):
        for k in range(2):
            for d in range(2):
                go(wcopy(d, 1, s, k))

    def wevent(s, h):
        for k in range(2):
            for d in range(2):
                hops = hop_counts(Z, k)[d]
                if h <= hops:
                    dst = wpart(s, zpeer(1 - d, h), k)
                    arrived(dst, dst, wsend.at[d, h - 1, s, k], wrecv.at[d, h - 1, s, k])
                    if h + 1 <= hops:
                        go(wcopy(d, h + 1, s, k))

    def rows_at(k, src_x, core, hf):
        return afull.at[(y + k) % Y, src_x * C + core, pl.ds(hf * (share // 2), share // 2)]

    def xcopy(d, h, k, hf):
        part = rows_at(k, xpeer(1 - d, h - 1), c, hf)
        return remote(part, part, xsend.at[d, h - 1, k, hf], xrecv.at[d, h - 1, k, hf], z, y, xpeer(d, 1), c)

    def ccopy(slot, k, hf):
        part = rows_at(k, (x + X - slot) % X, c, hf)
        return remote(part, part, csend.at[slot, k, hf], crecv.at[slot, k, hf], z, y, x, 1 - c)

    def yevent(k):
        part = afull.at[(y + k) % Y, t]
        arrived(part, part, ysend.at[Y - k], yrecv.at[Y - k])
        for hf in range(2):
            for d in range(2):
                go(xcopy(d, 1, k, hf))
        for hf in range(2):
            go(ccopy(0, k, hf))

    def xevent(h, k):
        for hf in range(2):
            for d in range(2):
                hops = hop_counts(X, hf)[d]
                if h <= hops:
                    part = rows_at(k, xpeer(1 - d, h), c, hf)
                    arrived(part, part, xsend.at[d, h - 1, k, hf], xrecv.at[d, h - 1, k, hf])
                    if h + 1 <= hops:
                        go(xcopy(d, h + 1, k, hf))
                    go(ccopy(h if d == 0 else X - h, k, hf))

    def cevent(j):
        slot = (X - ORIGINS[j]) % X
        for k in (1, 3, 2):
            for hf in range(2):
                part = rows_at(k, (x + ORIGINS[j]) % X, 1 - c, hf)
                arrived(part, part, csend.at[slot, k, hf], crecv.at[slot, k, hf])

    def inverse_of(slot):
        total = jnp.zeros((share, HEAD), jnp.float32)
        for i in range(features // 1024):
            h = staged[slot, :, i * 1024 : (i + 1) * 1024].astype(jnp.float32)
            h = h * h
            for u in range(1024 // HEAD):
                total += h[:, u * HEAD : (u + 1) * HEAD]
        return lax.rsqrt(jnp.sum(total, axis=1, keepdims=True) / features + epsilon)

    def normed(slot, inverse, zz, yy):
        parts = []
        for u in range(k_rows // HEAD):
            col = (zz * Y + yy) * (k_rows // HEAD) + u
            h = staged[slot, :, pl.ds(pl.multiple_of(col * HEAD, HEAD), HEAD)].astype(jnp.float32)
            parts.append((h * inverse * gain32[pl.ds(col, 1), :]).astype(jnp.bfloat16))
        return jnp.concatenate(parts, axis=1)

    def norm_own(i):
        slot = i % 2
        staging(i, slot).wait()
        inverse = inverse_of(slot)
        for zz in range(Z):
            afull[y, i, :, zz * k_rows : (zz + 1) * k_rows] = normed(slot, inverse, zz, y)
        if i + 2 < T:
            staging(i + 2, slot).start()

    def chip_of(j):
        return pl.ds(pl.multiple_of(((x + ORIGINS[j]) % X) * C, C), C)

    def project(s, j):
        @pl.loop(0, Y // 2)
        def _(i):
            owners = pl.ds(i * 2, 2)
            rows = afull[owners, chip_of(j)].reshape(2 * C * share, Z * k_rows)
            total = jnp.dot(rows, weights[s][...].reshape(Z * k_rows, Y * HEAD), preferred_element_type=jnp.float32)
            for d in range(Y):
                block = total[:, d * HEAD : (d + 1) * HEAD].reshape(2, C, share, HEAD)
                sums[s][d, owners, chip_of(j)] = block.astype(sums[s].dtype)
                if s == VALUES:
                    @pl.when(y == d)
                    def _():
                        vmine[owners, chip_of(j)] = block

    def reduce_begin(i):
        s, j = ORDER[i]
        for half, via in enumerate((1, Y - 1)):
            src = sums[s].at[(y + 2) % Y, pl.ds(half * 2, 2), chip_of(j)]
            dst = rs[s].at[1, pl.ds(half * 2, 2), chip_of(j)]
            go(remote(src, dst, rsend.at[s, 2 * half, j], rrecv.at[s, 2 * half, j], z, (y + via) % Y, x, c))

    def combine(i):
        s, j = ORDER[i]
        for half, k in enumerate((1, Y - 1)):
            owners = pl.ds(half * 2, 2)
            dst = rs[s].at[1, owners, chip_of(j)]
            arrived(dst, dst, rsend.at[s, 2 * half, j], rrecv.at[s, 2 * half, j])
            to = (y + k) % Y
            both = sums[s][to, owners, chip_of(j)].astype(jnp.float32) + rs[s][1, owners, chip_of(j)].astype(jnp.float32)
            sums[s][to, owners, chip_of(j)] = both.astype(sums[s].dtype)
            go(remote(sums[s].at[to, :, chip_of(j)], rs[s].at[k - 1, :, chip_of(j)], rsend.at[s, k, j], rrecv.at[s, k, j], z, to, x, c))

    def zcopy(d, h, s, j):
        dst = pages[s].at[zpeer(1 - d, h - 1), :, chip_of(j)]
        src = own[s].at[:, chip_of(j)] if h == 1 else dst
        return remote(src, dst, zsend.at[d, h - 1, s, j], zrecv.at[d, h - 1, s, j], zpeer(d, 1), y, x, c)

    def finish(i):
        s, j = ORDER[i]
        for k in (1, Y - 1):
            dst = rs[s].at[k - 1, :, chip_of(j)]
            arrived(dst, dst, rsend.at[s, k, j], rrecv.at[s, k, j])
        for m in range(Y):
            total = ksum[y, m, chip_of(j)] if s == KEYS else vmine[m, chip_of(j)]
            for k in (1, Y - 1):
                total += rs[s][k - 1, m, chip_of(j)].astype(jnp.float32)
            own[s][m, chip_of(j)] = total.astype(own[s].dtype)
        for d in range(2):
            go(zcopy(d, 1, s, j))
        local(own[s].at[:, chip_of(j)], pages[s].at[z, :, chip_of(j)])

    def pass_on(h, i):
        s, j = ORDER[i]
        for d in range(2):
            hops = hop_counts(Z, j)[d]
            if h <= hops:
                dst = pages[s].at[zpeer(1 - d, h), :, chip_of(j)]
                arrived(dst, dst, zsend.at[d, h - 1, s, j], zrecv.at[d, h - 1, s, j])
                if h + 1 <= hops:
                    go(zcopy(d, h + 1, s, j))

    pairs = q.shape[0] // 16

    def pages_of(r, pair):
        return [ids[r, 5, pair * 2], ids[r, 6, pair * 2], ids[r, 6, pair * 2 + 1]]

    def score(r):
        row = lax.broadcasted_iota(jnp.int32, (NBRS * GROUP, 1), 0)
        second = (row // 8) % 2 == 1

        @pl.loop(0, pairs, unroll=True)
        def _(pair):
            rows_q = qfull[r, :, pl.ds(pair * 16, 16), :].reshape(NBRS * GROUP, HEAD)
            scores = []
            for n, page in enumerate(pages_of(r, pair)):
                keys = kpages[page // 16, (page // 4) % 4, pl.ds((page % 4) * 2, 2)].reshape(2 * share, HEAD)
                s = lax.dot_general(rows_q, keys, (((1,), (1,)), ((), ())), preferred_element_type=jnp.float32)
                s = s * HEAD ** (-0.5)
                ok = mfull[page // 4, pl.ds(1 + page % 4, 1), :] != 0
                if n == 0:
                    ok = jnp.logical_and(ok, jnp.logical_not(second))
                elif n == 2:
                    ok = jnp.logical_and(ok, second)
                scores.append(jnp.where(ok, s, masked_score))
            s = jnp.concatenate(scores, axis=1)
            e = jnp.exp(s - jnp.max(s, axis=1, keepdims=True))
            probs[r, pair] = (e / jnp.sum(e, axis=1, keepdims=True)).astype(jnp.bfloat16)

    def mix(r):
        @pl.loop(0, pairs, unroll=True)
        def _(pair):
            values = [
                vpages[page // 16, (page // 4) % 4, pl.ds((page % 4) * 2, 2)].reshape(2 * share, HEAD)
                for page in pages_of(r, pair)
            ]
            mixed = jnp.dot(probs[r, pair], jnp.concatenate(values, axis=0), preferred_element_type=jnp.float32)
            ctx[r, :, pl.ds(pair * 16, 16), :] = mixed.astype(ctx.dtype).reshape(T, 16, HEAD)

    def head_cols(py, pt):
        return pl.ds(pl.multiple_of((pt * Y + py) * HEAD, HEAD), HEAD)

    def qcopy(k):
        p = (me + k) % (Y * T)
        py, pt = p // T, p % T
        return remote(q.at[:, head_cols(py, pt)], qfull.at[y, t], qsend.at[k], qrecv.at[k], z, py, pt // C, pt % C)

    def gcopy(ky, kt):
        py, pt = (y + ky) % Y, (t + kt) % T
        sem = ky * T + kt
        return remote(ctx.at[py, pt], out.at[:, head_cols(y, t)], gsend.at[sem], grecv.at[sem], z, py, pt // C, pt % C)

    def keep():
        totals = jnp.sum(mfull[:, 0, :], axis=0, keepdims=True)
        lane = lax.broadcasted_iota(jnp.int32, (1, meta.shape[1]), 1)
        slots = Y
        span = T // slots
        for m in range(Y):
            for slot in range(slots):
                at = pl.ds(slot * span, span)
                reads = jnp.sum(jnp.where(lane == (z * Y + m) * slots + slot, totals, 0), axis=1, keepdims=True)
                for s, masked in enumerate((kmask, vmask)):
                    rows = own[s][m, at].reshape(span * share, HEAD)
                    rows = jnp.where(reads > 0, rows, jnp.zeros_like(rows))
                    masked[m, slot * span * share : (slot + 1) * span * share] = rows
        for s, masked in enumerate((kmask, vmask)):
            for k in (2, 1, 3):
                m = (y + k) % Y
                go(remote(masked.at[m], kept[s].at[y], ksend.at[s, k], krecv.at[s, k], z, m, x, c))
            local(masked.at[y], kept[s].at[y])

    def ask():
        @pl.loop(1, Y * T)
        def _(k):
            qcopy(k).start()

        local(q.at[:, head_cols(y, t)], qfull.at[y, t])

    def tell():
        for k in (1, 3, 2):
            theirs = mfull.at[z * Y + (y + k) % Y]
            arrived(theirs, theirs, msend.at[Y - k], mrecv.at[Y - k])
        for k in range(1, Z):
            mine = mfull.at[pl.ds(z * Y, Y)]
            go(remote(mine, mine, nsend.at[k], nrecv.at[k], (z + k) % Z, y, x, c))

    def hear():
        for k in range(1, Z):
            theirs = mfull.at[pl.ds(((z + Z - k) % Z) * Y, Y)]
            arrived(theirs, theirs, nsend.at[k], nrecv.at[k])

    def told():
        local(mfull.at[pl.ds(z * Y, Y)], ids)

        @pl.loop(1, Y * T)
        def _(k):
            p = (me + Y * T - k) % (Y * T)
            part = qfull.at[p // T, p % T]
            arrived(part, part, qsend.at[k], qrecv.at[k])

    def settle():
        for cp in locals_[len(settled):]:
            cp.wait()
            settled.append(cp)

    settled = []

    staging(t, 0).start()
    greet_plane([((z + k) % Z, y, x, c) for k in range(1, Z)])
    wbegin(VALUES)
    for s in range(2):
        local(w.at[:, pl.ds(s * Y * HEAD, Y * HEAD)], weights[s].at[z])
    local(meta, mfull.at[z * Y + y])

    gain32[...] = gain[...].astype(jnp.float32)
    staging(t, 0).wait()
    inverse = inverse_of(0)
    for yy in range(Y):
        for zz in range(Z):
            act[yy, :, zz * k_rows : (zz + 1) * k_rows] = normed(0, inverse, zz, yy)
    for k in (1, 3, 2):
        dst = (y + k) % Y
        go(remote(act.at[dst], afull.at[y, t], ysend.at[k], yrecv.at[k], z, dst, x, c))
    for k in (1, 3, 2):
        go(remote(meta, mfull.at[z * Y + y], msend.at[k], mrecv.at[k], z, (y + k) % Y, x, c))
    for i in range(2):
        staging(i, i).start()

    w_, n_, x_, c_, p_ = wevent, norm_own, xevent, cevent, project
    start = [
        (w_, VALUES, 1), (n_, 0), (n_, 1), (yevent, 1), (yevent, 3), (w_, VALUES, 2),
        (n_, 2), (n_, 3), (yevent, 2), (n_, 4), (w_, VALUES, 3), (wbegin, KEYS), (x_, 1, 1), (n_, 5), (n_, 6), (n_, 7),
        (w_, VALUES, 4), (settle,), (c_, 0), (p_, VALUES, 0), (reduce_begin, 0), (ask,),
        (x_, 1, 3), (w_, KEYS, 1), (combine, 0), (x_, 1, 2), (c_, 1), (p_, VALUES, 1), (reduce_begin, 1),
        (w_, KEYS, 2), (c_, 2), (p_, VALUES, 2), (combine, 1), (finish, 0), (reduce_begin, 2),
        (w_, KEYS, 3), (x_, 2, 1), (combine, 2), (finish, 1), (pass_on, 1, 0), (w_, KEYS, 4),
        (p_, KEYS, 0), (reduce_begin, 3), (x_, 2, 3), (pass_on, 1, 1), (pass_on, 2, 0), (x_, 2, 2), (p_, KEYS, 1),
        (combine, 3), (finish, 2), (reduce_begin, 4),
        (pass_on, 2, 1), (pass_on, 3, 0), (c_, 3), (tell,), (p_, KEYS, 2),
    ]
    for f, *rest in start:
        f(*rest)
    work = [(project, KEYS, 3), (project, VALUES, 3)]
    n = len(ORDER)
    begun = 5
    done = {(1, 0), (2, 0), (1, 1), (2, 1), (3, 0)}
    for i in range(3, n + 4):
        if i < n:
            finish(i)
            while begun < min(n, i + 1 + WINDOW):
                reduce_begin(begun)
                begun += 1
        for h in (1, 2, 3, 4):
            k = i - h
            if 0 <= k < n and (h, k) not in done:
                pass_on(h, k)
                done.add((h, k))
            if h == 2 and i + 1 < n:
                combine(i + 1)
            if work and (h == 3 or k > KEYS_DONE):
                f, *rest = work.pop(0)
                f(*rest)
            if (h, k) == (4, KEYS_DONE):
                told()
                settle()
                work += [(score, r) for r in range(Y)]
            if (h, k) == (1, n - 1):
                hear()
                keep()
    for f, *rest in work:
        f(*rest)
    settle()

    for ky in (2, 1, 3, 0):
        mix((y + ky) % Y)

        @pl.loop(0 if ky else 1, T)
        def _(kt):
            gcopy(ky, kt).start()

    last = pltpu.make_async_copy(ctx.at[y, t], out.at[:, head_cols(y, t)], lsem.at[len(locals_)])
    last.start()
    for s in range(2):
        for k in range(1, Y):
            part = kept[s].at[(y + Y - k) % Y]
            arrived(part, part, ksend.at[s, k], krecv.at[s, k])
    for cp in sends:
        cp.wait_send()

    @pl.loop(1, Y * T)
    def _(k):
        qcopy(k).wait_send()

    for ky in (2, 1, 3, 0):
        @pl.loop(0 if ky else 1, T)
        def _(kt):
            sem = ky * T + kt
            cols = head_cols((y + Y - ky) % Y, (t + T - kt) % T)
            arrived(ctx.at[y, t], out.at[:, cols], gsend.at[sem], grecv.at[sem])
            gcopy(ky, kt).wait_send()

    last.wait()
    settle()


def layer(enc, gain, w, q, meta):
    dma = pltpu.SemaphoreType.DMA
    bf16, f32 = jnp.bfloat16, jnp.float32
    share = enc.shape[0] // T
    k_rows = w.shape[0]
    depth = Z * k_rows
    block = (Y, T, share, HEAD)
    hbm = pl.BlockSpec(memory_space=pl.ANY)
    kept = jax.ShapeDtypeStruct((Y, T * share, HEAD), bf16)
    pairs = q.shape[0] // 16
    return pl.pallas_call(
        layer_kernel,
        out_shape=(
            jax.ShapeDtypeStruct(q.shape, bf16),
            kept,
            kept,
        ),
        in_specs=[hbm, pl.BlockSpec(memory_space=pltpu.VMEM), hbm, hbm, hbm],
        out_specs=[hbm] * 3,
        scratch_shapes=[
            pltpu.VMEM(gain.shape, f32),
            pltpu.VMEM((2, share, enc.shape[1]), bf16),
            pltpu.VMEM((Y, share, depth), bf16),
            pltpu.VMEM((Y, T, share, depth), bf16),
            pltpu.VMEM((Z, k_rows, Y * HEAD), bf16),
            pltpu.VMEM((Z, k_rows, Y * HEAD), bf16),
            pltpu.VMEM((Y,) + block, f32),
            pltpu.VMEM((Y,) + block, bf16),
            pltpu.VMEM(block, f32),
            pltpu.VMEM((Y - 1,) + block, f32),
            pltpu.VMEM((Y - 1,) + block, bf16),
            pltpu.VMEM(block, bf16),
            pltpu.VMEM(block, bf16),
            pltpu.VMEM((Z,) + block, bf16),
            pltpu.VMEM((Z,) + block, bf16),
            pltpu.VMEM((Y, T, q.shape[0], HEAD), bf16),
            pltpu.VMEM((Y, pairs, NBRS * GROUP, 3 * HEAD), bf16),
            pltpu.VMEM((Y, T, q.shape[0], HEAD), bf16),
            pltpu.VMEM((Z * Y,) + meta.shape, meta.dtype),
            pltpu.SMEM((Y,) + meta.shape, meta.dtype),
            pltpu.VMEM((Y, T * share, HEAD), bf16),
            pltpu.VMEM((Y, T * share, HEAD), bf16),
            dma((24,)),
            dma((2,)),
            dma((2, Z // 2, 2, 2)), dma((2, Z // 2, 2, 2)),
            dma((Y,)), dma((Y,)),
            dma((2, X // 2, Y, 2)), dma((2, X // 2, Y, 2)),
            dma((X, Y, 2)), dma((X, Y, 2)),
            dma((Y * T,)), dma((Y * T,)),
            dma((Y,)), dma((Y,)),
            dma((Z,)), dma((Z,)),
            dma((2, Y, X)), dma((2, Y, X)),
            dma((2, Z // 2, 2, X)), dma((2, Z // 2, 2, X)),
            dma((2, Y)), dma((2, Y)),
            dma((Y * T,)), dma((Y * T,)),
        ],
        compiler_params=pltpu.CompilerParams(
            has_side_effects=True, collective_id=1, vmem_limit_bytes=60 * 2**20
        ),
        name="layer",
    )(enc, gain, w, q, meta)


def shards(
    queries, enc_hidden, enc_gain, kv_weight, neighbour_pages, reader_counts, neighbour_tokens
):
    pages_here, nb_tokens, features = enc_hidden.shape
    groups_here = queries.shape[0]
    k_rows = kv_weight.shape[0]
    rows_here = pages_here * nb_tokens
    w = kv_weight.reshape(k_rows, -1)

    ids = neighbour_pages.T
    facts = jnp.concatenate(
        [reader_counts, neighbour_tokens, jnp.pad(ids, ((0, 1), (0, nb_tokens - groups_here)))]
    )
    context, kkept, vkept = layer(
        enc_hidden.reshape(rows_here, features),
        enc_gain.reshape(-1, HEAD),
        w,
        queries.reshape(-1, queries.shape[2]),
        facts,
    )
    kept = jnp.stack([kkept, vkept]).reshape(2, Y, pages_here, nb_tokens, HEAD).transpose(2, 3, 0, 1, 4)
    kept_pages = kept.reshape(pages_here, nb_tokens, 2, Y * HEAD)
    return (context.reshape(queries.shape), kept_pages)


def solution(mesh):
    placed = (
        P("dp", "tensor", None),
        P("dp", None, None),
        P(),
        P("dp", None, "tensor"),
        P("dp", None),
        P("dp", None),
        P("dp", None),
    )
    return jax.shard_map(
        shards,
        mesh=mesh,
        in_specs=placed,
        out_specs=(P("dp", "tensor", None), P("dp", None, None, "tensor")),
        check_vma=False,
    )
```

```python
import functools

import jax
import jax.numpy as jnp
from jax import lax
from jax.experimental import pallas as pl
from jax.experimental.pallas import tpu as pltpu
from jax.sharding import PartitionSpec as P

HEAD = 128
GROUP = 64
NBRS = 2
Z, Y, X, C = 8, 4, 4, 2
T = X * C
MESH = pl.DeviceIdType.MESH

epsilon = 1e-05
masked_score = -1e30


def place():
    dp = lax.axis_index("dp")
    t = lax.axis_index("tensor")
    return dp // Y, dp % Y, t // C, t % C


def remote(src, dst, send, recv, z, y, x, c):
    return pltpu.make_async_remote_copy(
        src_ref=src,
        dst_ref=dst,
        send_sem=send,
        recv_sem=recv,
        device_id=(z * Y + y, x * C + c),
        device_id_type=MESH,
    )


def greet_plane(also=()):
    z, y, x, c = place()
    me = y * T + x * C + c
    barrier = pltpu.get_barrier_semaphore()

    @pl.loop(1, Y * T)
    def _(k):
        p = (me + k) % (Y * T)
        pl.semaphore_signal(barrier, inc=1, device_id=(z * Y + p // T, p % T), device_id_type=MESH)

    for pz, py, px, pc in also:
        pl.semaphore_signal(barrier, inc=1, device_id=(pz * Y + py, px * C + pc), device_id_type=MESH)
    pl.semaphore_wait(barrier, Y * T - 1 + len(also))


def hop_counts(n, c):
    far, near = n // 2, n - 1 - n // 2
    return (far, near) if c % 2 == 0 else (near, far)


KEYS, VALUES = 0, 1
ORIGINS = (0, 1, 3, 2)
ORDER = [(VALUES, j) for j in range(X - 1)] + [(KEYS, j) for j in range(X)] + [(VALUES, X - 1)]
KEYS_DONE = 6
WINDOW = 2


def layer_kernel(
    enc, gain, w, q, meta, out, kkept, vkept,
    gain32, staged, act, afull, wk, wv, ksum, vsum, vmine, krs, vrs, kown, vown, kpages, vpages,
    qfull, probs, ctx, mfull, ids, kmask, vmask,
    lsem, ssem, wsend, wrecv, ysend, yrecv, xsend, xrecv, csend, crecv, qsend, qrecv,
    msend, mrecv, nsend, nrecv, rsend, rrecv, zsend, zrecv, ksend, krecv, gsend, grecv,
):
    z, y, x, c = place()
    t = x * C + c
    me = y * T + t
    share = act.shape[1]
    k_rows = wk.shape[1]
    features = enc.shape[1]
    weights, sums, rs = (wk, wv), (ksum, vsum), (krs, vrs)
    own, pages, kept = (kown, vown), (kpages, vpages), (kkept, vkept)
    locals_ = []
    sends = []

    def local(src, dst):
        cp = pltpu.make_async_copy(src, dst, lsem.at[len(locals_)])
        cp.start()
        locals_.append(cp)
        return cp

    def go(cp):
        cp.start()
        sends.append(cp)

    def arrived(src, dst, send, recv):
        remote(src, dst, send, recv, z, y, x, 1 - c).wait_recv()

    def zpeer(d, h):
        return (z + h) % Z if d == 0 else (z + Z - h) % Z

    def xpeer(d, h):
        return (x + h) % X if d == 0 else (x + X - h) % X

    def staging(i, slot):
        rows = pl.ds(pl.multiple_of(i * share, share), share)
        return pltpu.make_async_copy(enc.at[rows], staged.at[slot], ssem.at[slot])

    half = k_rows // 2

    def wpart(s, src_z, k):
        return weights[s].at[src_z, pl.ds(k * half, half)]

    def wcopy(d, h, s, k):
        dst = wpart(s, zpeer(1 - d, h - 1), k)
        src = w.at[pl.ds(k * half, half), pl.ds(s * Y * HEAD, Y * HEAD)] if h == 1 else dst
        return remote(src, dst, wsend.at[d, h - 1, s, k], wrecv.at[d, h - 1, s, k], zpeer(d, 1), y, x, c)

    def wbegin(s):
        for k in range(2):
            for d in range(2):
                go(wcopy(d, 1, s, k))

    def wevent(s, h):
        for k in range(2):
            for d in range(2):
                hops = hop_counts(Z, k)[d]
                if h <= hops:
                    dst = wpart(s, zpeer(1 - d, h), k)
                    arrived(dst, dst, wsend.at[d, h - 1, s, k], wrecv.at[d, h - 1, s, k])
                    if h + 1 <= hops:
                        go(wcopy(d, h + 1, s, k))

    def rows_at(k, src_x, core, hf):
        return afull.at[(y + k) % Y, src_x * C + core, pl.ds(hf * (share // 2), share // 2)]

    def xcopy(d, h, k, hf):
        part = rows_at(k, xpeer(1 - d, h - 1), c, hf)
        return remote(part, part, xsend.at[d, h - 1, k, hf], xrecv.at[d, h - 1, k, hf], z, y, xpeer(d, 1), c)

    def ccopy(slot, k, hf):
        part = rows_at(k, (x + X - slot) % X, c, hf)
        return remote(part, part, csend.at[slot, k, hf], crecv.at[slot, k, hf], z, y, x, 1 - c)

    def yevent(k):
        part = afull.at[(y + k) % Y, t]
        arrived(part, part, ysend.at[Y - k], yrecv.at[Y - k])
        for hf in range(2):
            for d in range(2):
                go(xcopy(d, 1, k, hf))
        for hf in range(2):
            go(ccopy(0, k, hf))

    def xevent(h, k):
        for hf in range(2):
            for d in range(2):
                hops = hop_counts(X, hf)[d]
                if h <= hops:
                    part = rows_at(k, xpeer(1 - d, h), c, hf)
                    arrived(part, part, xsend.at[d, h - 1, k, hf], xrecv.at[d, h - 1, k, hf])
                    if h + 1 <= hops:
                        go(xcopy(d, h + 1, k, hf))
                    go(ccopy(h if d == 0 else X - h, k, hf))

    def cevent(j):
        slot = (X - ORIGINS[j]) % X
        for k in (1, 3, 2):
            for hf in range(2):
                part = rows_at(k, (x + ORIGINS[j]) % X, 1 - c, hf)
                arrived(part, part, csend.at[slot, k, hf], crecv.at[slot, k, hf])

    def inverse_of(slot):
        total = jnp.zeros((share, HEAD), jnp.float32)
        for i in range(features // 1024):
            h = staged[slot, :, i * 1024 : (i + 1) * 1024].astype(jnp.float32)
            h = h * h
            for u in range(1024 // HEAD):
                total += h[:, u * HEAD : (u + 1) * HEAD]
        return lax.rsqrt(jnp.sum(total, axis=1, keepdims=True) / features + epsilon)

    def normed(slot, inverse, zz, yy):
        parts = []
        for u in range(k_rows // HEAD):
            col = (zz * Y + yy) * (k_rows // HEAD) + u
            h = staged[slot, :, pl.ds(pl.multiple_of(col * HEAD, HEAD), HEAD)].astype(jnp.float32)
            parts.append((h * inverse * gain32[pl.ds(col, 1), :]).astype(jnp.bfloat16))
        return jnp.concatenate(parts, axis=1)

    def norm_own(i):
        slot = i % 2
        staging(i, slot).wait()
        inverse = inverse_of(slot)
        for zz in range(Z):
            afull[y, i, :, zz * k_rows : (zz + 1) * k_rows] = normed(slot, inverse, zz, y)
        if i + 2 < T:
            staging(i + 2, slot).start()

    def chip_of(j):
        return pl.ds(pl.multiple_of(((x + ORIGINS[j]) % X) * C, C), C)

    def project(s, j):
        @pl.loop(0, Y // 2)
        def _(i):
            owners = pl.ds(i * 2, 2)
            rows = afull[owners, chip_of(j)].reshape(2 * C * share, Z * k_rows)
            total = jnp.dot(rows, weights[s][...].reshape(Z * k_rows, Y * HEAD), preferred_element_type=jnp.float32)
            for d in range(Y):
                block = total[:, d * HEAD : (d + 1) * HEAD].reshape(2, C, share, HEAD)
                sums[s][d, owners, chip_of(j)] = block.astype(sums[s].dtype)
                if s == VALUES:
                    @pl.when(y == d)
                    def _():
                        vmine[owners, chip_of(j)] = block

    def reduce_begin(i):
        s, j = ORDER[i]
        for k in (2, 1, 3):
            dst = (y + k) % Y
            go(remote(sums[s].at[dst, :, chip_of(j)], rs[s].at[k - 1, :, chip_of(j)], rsend.at[s, k, j], rrecv.at[s, k, j], z, dst, x, c))

    def zcopy(d, h, s, j):
        dst = pages[s].at[zpeer(1 - d, h - 1), :, chip_of(j)]
        src = own[s].at[:, chip_of(j)] if h == 1 else dst
        return remote(src, dst, zsend.at[d, h - 1, s, j], zrecv.at[d, h - 1, s, j], zpeer(d, 1), y, x, c)

    def finish(i):
        s, j = ORDER[i]
        for k in (1, 3, 2):
            dst = rs[s].at[k - 1, :, chip_of(j)]
            arrived(dst, dst, rsend.at[s, k, j], rrecv.at[s, k, j])
        for m in range(Y):
            total = ksum[y, m, chip_of(j)] if s == KEYS else vmine[m, chip_of(j)]
            for k in range(1, Y):
                total += rs[s][k - 1, m, chip_of(j)].astype(jnp.float32)
            own[s][m, chip_of(j)] = total.astype(own[s].dtype)
        for d in range(2):
            go(zcopy(d, 1, s, j))
        local(own[s].at[:, chip_of(j)], pages[s].at[z, :, chip_of(j)])

    def pass_on(h, i):
        s, j = ORDER[i]
        for d in range(2):
            hops = hop_counts(Z, j)[d]
            if h <= hops:
                dst = pages[s].at[zpeer(1 - d, h), :, chip_of(j)]
                arrived(dst, dst, zsend.at[d, h - 1, s, j], zrecv.at[d, h - 1, s, j])
                if h + 1 <= hops:
                    go(zcopy(d, h + 1, s, j))

    pairs = q.shape[0] // 16

    def pages_of(r, pair):
        return [ids[r, 5, pair * 2], ids[r, 6, pair * 2], ids[r, 6, pair * 2 + 1]]

    def score(r):
        row = lax.broadcasted_iota(jnp.int32, (NBRS * GROUP, 1), 0)
        second = (row // 8) % 2 == 1

        @pl.loop(0, pairs, unroll=True)
        def _(pair):
            rows_q = qfull[r, :, pl.ds(pair * 16, 16), :].reshape(NBRS * GROUP, HEAD)
            scores = []
            for n, page in enumerate(pages_of(r, pair)):
                keys = kpages[page // 16, (page // 4) % 4, pl.ds((page % 4) * 2, 2)].reshape(2 * share, HEAD)
                s = lax.dot_general(rows_q, keys, (((1,), (1,)), ((), ())), preferred_element_type=jnp.float32)
                s = s * HEAD ** (-0.5)
                ok = mfull[page // 4, pl.ds(1 + page % 4, 1), :] != 0
                if n == 0:
                    ok = jnp.logical_and(ok, jnp.logical_not(second))
                elif n == 2:
                    ok = jnp.logical_and(ok, second)
                scores.append(jnp.where(ok, s, masked_score))
            s = jnp.concatenate(scores, axis=1)
            e = jnp.exp(s - jnp.max(s, axis=1, keepdims=True))
            probs[r, pair] = (e / jnp.sum(e, axis=1, keepdims=True)).astype(jnp.bfloat16)

    def mix(r):
        @pl.loop(0, pairs, unroll=True)
        def _(pair):
            values = [
                vpages[page // 16, (page // 4) % 4, pl.ds((page % 4) * 2, 2)].reshape(2 * share, HEAD)
                for page in pages_of(r, pair)
            ]
            mixed = jnp.dot(probs[r, pair], jnp.concatenate(values, axis=0), preferred_element_type=jnp.float32)
            ctx[r, :, pl.ds(pair * 16, 16), :] = mixed.astype(ctx.dtype).reshape(T, 16, HEAD)

    def head_cols(py, pt):
        return pl.ds(pl.multiple_of((pt * Y + py) * HEAD, HEAD), HEAD)

    def qcopy(k):
        p = (me + k) % (Y * T)
        py, pt = p // T, p % T
        return remote(q.at[:, head_cols(py, pt)], qfull.at[y, t], qsend.at[k], qrecv.at[k], z, py, pt // C, pt % C)

    def gcopy(ky, kt):
        py, pt = (y + ky) % Y, (t + kt) % T
        sem = ky * T + kt
        return remote(ctx.at[py, pt], out.at[:, head_cols(y, t)], gsend.at[sem], grecv.at[sem], z, py, pt // C, pt % C)

    def keep():
        totals = jnp.sum(mfull[:, 0, :], axis=0, keepdims=True)
        lane = lax.broadcasted_iota(jnp.int32, (1, meta.shape[1]), 1)
        slots = Y
        span = T // slots
        for m in range(Y):
            for slot in range(slots):
                at = pl.ds(slot * span, span)
                reads = jnp.sum(jnp.where(lane == (z * Y + m) * slots + slot, totals, 0), axis=1, keepdims=True)
                for s, masked in enumerate((kmask, vmask)):
                    rows = own[s][m, at].reshape(span * share, HEAD)
                    rows = jnp.where(reads > 0, rows, jnp.zeros_like(rows))
                    masked[m, slot * span * share : (slot + 1) * span * share] = rows
        for s, masked in enumerate((kmask, vmask)):
            for k in (2, 1, 3):
                m = (y + k) % Y
                go(remote(masked.at[m], kept[s].at[y], ksend.at[s, k], krecv.at[s, k], z, m, x, c))
            local(masked.at[y], kept[s].at[y])

    def ask():
        @pl.loop(1, Y * T)
        def _(k):
            qcopy(k).start()

        local(q.at[:, head_cols(y, t)], qfull.at[y, t])

    def tell():
        for k in (1, 3, 2):
            theirs = mfull.at[z * Y + (y + k) % Y]
            arrived(theirs, theirs, msend.at[Y - k], mrecv.at[Y - k])
        for k in range(1, Z):
            mine = mfull.at[pl.ds(z * Y, Y)]
            go(remote(mine, mine, nsend.at[k], nrecv.at[k], (z + k) % Z, y, x, c))

    def hear():
        for k in range(1, Z):
            theirs = mfull.at[pl.ds(((z + Z - k) % Z) * Y, Y)]
            arrived(theirs, theirs, nsend.at[k], nrecv.at[k])

    def told():
        local(mfull.at[pl.ds(z * Y, Y)], ids)

        @pl.loop(1, Y * T)
        def _(k):
            p = (me + Y * T - k) % (Y * T)
            part = qfull.at[p // T, p % T]
            arrived(part, part, qsend.at[k], qrecv.at[k])

    def settle():
        for cp in locals_[len(settled):]:
            cp.wait()
            settled.append(cp)

    settled = []

    staging(t, 0).start()
    greet_plane([((z + k) % Z, y, x, c) for k in range(1, Z)])
    wbegin(VALUES)
    for s in range(2):
        local(w.at[:, pl.ds(s * Y * HEAD, Y * HEAD)], weights[s].at[z])
    local(meta, mfull.at[z * Y + y])

    gain32[...] = gain[...].astype(jnp.float32)
    staging(t, 0).wait()
    inverse = inverse_of(0)
    for yy in range(Y):
        for zz in range(Z):
            act[yy, :, zz * k_rows : (zz + 1) * k_rows] = normed(0, inverse, zz, yy)
    for k in (1, 3, 2):
        dst = (y + k) % Y
        go(remote(act.at[dst], afull.at[y, t], ysend.at[k], yrecv.at[k], z, dst, x, c))
    for k in (1, 3, 2):
        go(remote(meta, mfull.at[z * Y + y], msend.at[k], mrecv.at[k], z, (y + k) % Y, x, c))
    for i in range(2):
        staging(i, i).start()

    w_, n_, x_, c_, p_ = wevent, norm_own, xevent, cevent, project
    start = [
        (w_, VALUES, 1), (n_, 0), (n_, 1), (yevent, 1), (yevent, 3), (w_, VALUES, 2),
        (n_, 2), (n_, 3), (yevent, 2), (n_, 4), (w_, VALUES, 3), (wbegin, KEYS), (x_, 1, 1), (n_, 5), (n_, 6), (n_, 7),
        (w_, VALUES, 4), (settle,), (c_, 0), (p_, VALUES, 0), (reduce_begin, 0), (ask,),
        (x_, 1, 3), (w_, KEYS, 1), (x_, 1, 2), (c_, 1), (p_, VALUES, 1), (reduce_begin, 1),
        (w_, KEYS, 2), (c_, 2), (p_, VALUES, 2), (finish, 0), (reduce_begin, 2),
        (w_, KEYS, 3), (x_, 2, 1), (finish, 1), (pass_on, 1, 0), (w_, KEYS, 4), (p_, KEYS, 0), (reduce_begin, 3),
        (x_, 2, 3), (pass_on, 1, 1), (pass_on, 2, 0), (x_, 2, 2), (p_, KEYS, 1), (finish, 2), (reduce_begin, 4),
        (pass_on, 2, 1), (pass_on, 3, 0), (c_, 3), (tell,), (p_, KEYS, 2),
    ]
    for f, *rest in start:
        f(*rest)
    work = [(project, KEYS, 3), (project, VALUES, 3)]
    n = len(ORDER)
    begun = 5
    done = {(1, 0), (2, 0), (1, 1), (2, 1), (3, 0)}
    for i in range(3, n + 4):
        if i < n:
            finish(i)
            while begun < min(n, i + 1 + WINDOW):
                reduce_begin(begun)
                begun += 1
        for h in (1, 2, 3, 4):
            k = i - h
            if 0 <= k < n and (h, k) not in done:
                pass_on(h, k)
                done.add((h, k))
            if work and (h == 3 or k > KEYS_DONE):
                f, *rest = work.pop(0)
                f(*rest)
            if (h, k) == (4, KEYS_DONE):
                told()
                settle()
                work += [(score, r) for r in range(Y)]
            if (h, k) == (1, n - 1):
                hear()
                keep()
    for f, *rest in work:
        f(*rest)
    settle()

    for ky in (2, 1, 3, 0):
        mix((y + ky) % Y)

        @pl.loop(0 if ky else 1, T)
        def _(kt):
            gcopy(ky, kt).start()

    last = pltpu.make_async_copy(ctx.at[y, t], out.at[:, head_cols(y, t)], lsem.at[len(locals_)])
    last.start()
    for s in range(2):
        for k in range(1, Y):
            part = kept[s].at[(y + Y - k) % Y]
            arrived(part, part, ksend.at[s, k], krecv.at[s, k])
    for cp in sends:
        cp.wait_send()

    @pl.loop(1, Y * T)
    def _(k):
        qcopy(k).wait_send()

    for ky in (2, 1, 3, 0):
        @pl.loop(0 if ky else 1, T)
        def _(kt):
            sem = ky * T + kt
            cols = head_cols((y + Y - ky) % Y, (t + T - kt) % T)
            arrived(ctx.at[y, t], out.at[:, cols], gsend.at[sem], grecv.at[sem])
            gcopy(ky, kt).wait_send()

    last.wait()
    settle()


def layer(enc, gain, w, q, meta):
    dma = pltpu.SemaphoreType.DMA
    bf16, f32 = jnp.bfloat16, jnp.float32
    share = enc.shape[0] // T
    k_rows = w.shape[0]
    depth = Z * k_rows
    block = (Y, T, share, HEAD)
    hbm = pl.BlockSpec(memory_space=pl.ANY)
    kept = jax.ShapeDtypeStruct((Y, T * share, HEAD), bf16)
    pairs = q.shape[0] // 16
    return pl.pallas_call(
        layer_kernel,
        out_shape=(
            jax.ShapeDtypeStruct(q.shape, bf16),
            kept,
            kept,
        ),
        in_specs=[hbm, pl.BlockSpec(memory_space=pltpu.VMEM), hbm, hbm, hbm],
        out_specs=[hbm] * 3,
        scratch_shapes=[
            pltpu.VMEM(gain.shape, f32),
            pltpu.VMEM((2, share, enc.shape[1]), bf16),
            pltpu.VMEM((Y, share, depth), bf16),
            pltpu.VMEM((Y, T, share, depth), bf16),
            pltpu.VMEM((Z, k_rows, Y * HEAD), bf16),
            pltpu.VMEM((Z, k_rows, Y * HEAD), bf16),
            pltpu.VMEM((Y,) + block, f32),
            pltpu.VMEM((Y,) + block, bf16),
            pltpu.VMEM(block, f32),
            pltpu.VMEM((Y - 1,) + block, f32),
            pltpu.VMEM((Y - 1,) + block, bf16),
            pltpu.VMEM(block, bf16),
            pltpu.VMEM(block, bf16),
            pltpu.VMEM((Z,) + block, bf16),
            pltpu.VMEM((Z,) + block, bf16),
            pltpu.VMEM((Y, T, q.shape[0], HEAD), bf16),
            pltpu.VMEM((Y, pairs, NBRS * GROUP, 3 * HEAD), bf16),
            pltpu.VMEM((Y, T, q.shape[0], HEAD), bf16),
            pltpu.VMEM((Z * Y,) + meta.shape, meta.dtype),
            pltpu.SMEM((Y,) + meta.shape, meta.dtype),
            pltpu.VMEM((Y, T * share, HEAD), bf16),
            pltpu.VMEM((Y, T * share, HEAD), bf16),
            dma((24,)),
            dma((2,)),
            dma((2, Z // 2, 2, 2)), dma((2, Z // 2, 2, 2)),
            dma((Y,)), dma((Y,)),
            dma((2, X // 2, Y, 2)), dma((2, X // 2, Y, 2)),
            dma((X, Y, 2)), dma((X, Y, 2)),
            dma((Y * T,)), dma((Y * T,)),
            dma((Y,)), dma((Y,)),
            dma((Z,)), dma((Z,)),
            dma((2, Y, X)), dma((2, Y, X)),
            dma((2, Z // 2, 2, X)), dma((2, Z // 2, 2, X)),
            dma((2, Y)), dma((2, Y)),
            dma((Y * T,)), dma((Y * T,)),
        ],
        compiler_params=pltpu.CompilerParams(
            has_side_effects=True, collective_id=1, vmem_limit_bytes=60 * 2**20
        ),
        name="layer",
    )(enc, gain, w, q, meta)


def shards(
    queries, enc_hidden, enc_gain, kv_weight, neighbour_pages, reader_counts, neighbour_tokens
):
    pages_here, nb_tokens, features = enc_hidden.shape
    groups_here = queries.shape[0]
    k_rows = kv_weight.shape[0]
    rows_here = pages_here * nb_tokens
    w = kv_weight.reshape(k_rows, -1)

    ids = neighbour_pages.T
    facts = jnp.concatenate(
        [reader_counts, neighbour_tokens, jnp.pad(ids, ((0, 1), (0, nb_tokens - groups_here)))]
    )
    context, kkept, vkept = layer(
        enc_hidden.reshape(rows_here, features),
        enc_gain.reshape(-1, HEAD),
        w,
        queries.reshape(-1, queries.shape[2]),
        facts,
    )
    kept = jnp.stack([kkept, vkept]).reshape(2, Y, pages_here, nb_tokens, HEAD).transpose(2, 3, 0, 1, 4)
    kept_pages = kept.reshape(pages_here, nb_tokens, 2, Y * HEAD)
    return (context.reshape(queries.shape), kept_pages)


def solution(mesh):
    placed = (
        P("dp", "tensor", None),
        P("dp", None, None),
        P(),
        P("dp", None, "tensor"),
        P("dp", None),
        P("dp", None),
        P("dp", None),
    )
    return jax.shard_map(
        shards,
        mesh=mesh,
        in_specs=placed,
        out_specs=(P("dp", "tensor", None), P("dp", None, None, "tensor")),
        check_vma=False,
    )
```
